256 devices in a mesh: rows: 8 (over x, core), cols: 32 (over z, y).
Axes of the slice: x: 4, y: 4, z: 8, core: 2. Of those that a mesh axis runs over, the one named last changes fastest.
Arguments:
- sinogram: float32 [8, 131072], P(None, ('rows', 'cols'))
- tiles: bfloat16 [8, 20480, 4096], P('rows', 'cols'), may hold values from -0.375 to 0.375
- tile_rows: int32 [8, 20480], P('rows', 'cols'), may hold values from 0 to 255
- tile_cols: int32 [8, 20480], P('rows', 'cols'), may hold values from 0 to 511
- tile_counts: int32 [8, 32], P('rows', 'cols'), may hold values from 1 to 640, as said below
Outputs:
- solution: float32 [8, 1048576], P(None, ('cols', 'rows'))
- residual: float32 [8, 131072], P(None, ('rows', 'cols'))
- gradient: float32 [8, 1048576], P(None, ('cols', 'rows'))
The draws below stay inside these ranges and needn't reach their ends.
Inputs may be any that keep to these rules, and one draw needn't show every extreme that they name: tile_counts[i][j] is the number of live slots of device (i, j); slots from it on hold unused tiles; in every draw some device has all 640 slots live.
All inputs are finite; a program needn't handle non-finite values.
Results may differ from the reference program's by a relative error of at most 0.04.
Values may be sent and summed in bfloat16 or wider, within the bound.
A program may use at most 64 MiB of HBM per device.

```python
import jax
import jax.numpy as jnp
from jax import lax

SLICES = 8
TILE = 64
RT_DEV = 256
PT_DEV = 512
TILES_DEV = 640
ITERS = 2
NRAY = 131072
NPIX = 1048576
SLOTS = 20480
N_ROWS = 8
N_COLS = 32


def draw_sinogram(key, part):
    key = jax.random.fold_in(key, 11)
    first = jax.random.fold_in(key, 0)
    ramp = 1.0 + 2.0 * jnp.arange(NRAY, dtype=jnp.float32) / NRAY
    base = jax.random.normal(first, (SLICES, NRAY), jnp.float32)
    return (base * ramp[None, :]).astype(jnp.float32)


def draw_tile_counts(key, part):
    key = jax.random.fold_in(key, 23)
    first, second = jax.random.split(key)
    level = jax.random.randint(first, (N_ROWS * N_COLS,), 8, 65)
    counts = jnp.maximum(1, TILES_DEV * level * level // 4096)
    busiest = jax.random.randint(second, (), 0, N_ROWS * N_COLS)
    counts = counts.at[busiest].set(TILES_DEV)
    return counts.reshape(N_ROWS, N_COLS).astype(jnp.int32)


def place_ends(values, key, least, largest):
    place = [jax.random.randint(jax.random.fold_in(key, axis), (), 0, length) for axis, length in enumerate(values.shape)]
    main_axis = values.shape.index(max(values.shape))
    beside = place[:main_axis] + [(place[main_axis] + 1) % values.shape[main_axis]] + place[main_axis + 1:]
    return values.at[tuple(place)].set(least).at[tuple(beside)].set(largest)


def level_of(rng, dims, pieces, smallest, largest):
    gain = 1.0
    for position, parts in pieces:
        draws = jax.random.uniform(jax.random.fold_in(jax.random.fold_in(rng, 6), position), (parts,), jnp.float32, smallest / len(pieces), largest / len(pieces))
        gain = gain * jnp.repeat(jnp.exp(draws), dims[position] // parts).reshape((-1,) + (1,) * (len(dims) - 1 - position))
    return gain


def noise(own_key, extent, scale, reach, cuts=(), kind=jnp.bfloat16):
    loudness = level_of(own_key, extent, cuts, -0.22, 0.18) if cuts else 1.0
    drawn = jax.random.normal(own_key, extent, jnp.float32) * scale * loudness
    return jnp.minimum(jnp.maximum(drawn, -reach), reach).astype(kind)


def setup_inputs(seed: int = 0) -> dict:
    arg_keys = jax.random.split(jax.random.key(seed), 6)
    return {
        "sinogram": draw_sinogram(jax.random.fold_in(arg_keys[5], 71), 0),
        "tiles": noise(arg_keys[1], (N_ROWS, SLOTS, TILE * TILE), (4 * TILE) ** -0.5, 0.375, ((0, 8), (1, 32))),
        "tile_rows": place_ends(jax.random.randint(arg_keys[2], (N_ROWS, SLOTS), 0, RT_DEV), jax.random.fold_in(arg_keys[2], 1), 0, RT_DEV - 1).astype(jnp.int32),
        "tile_cols": place_ends(jax.random.randint(arg_keys[3], (N_ROWS, SLOTS), 0, PT_DEV), jax.random.fold_in(arg_keys[3], 1), 0, PT_DEV - 1).astype(jnp.int32),
        "tile_counts": draw_tile_counts(jax.random.fold_in(arg_keys[5], 71), 0),
    }


def rounded(values):
    return lax.optimization_barrier(values.astype(jnp.bfloat16)).astype(jnp.float32)


def device_slots(tiles, tile_rows, tile_cols, tile_counts, device):
    row_group = device // N_COLS
    col_group = device % N_COLS
    start = (col_group * TILES_DEV).astype(jnp.int32)
    group_tiles = lax.dynamic_index_in_dim(tiles, row_group, 0, keepdims=False)
    plates = lax.dynamic_slice_in_dim(group_tiles, start, TILES_DEV, 0)
    plates = plates.astype(jnp.float32).reshape(TILES_DEV, TILE, TILE)
    row_ids = lax.dynamic_slice_in_dim(lax.dynamic_index_in_dim(tile_rows, row_group, 0, keepdims=False), start, TILES_DEV, 0)
    column_ids = lax.dynamic_slice_in_dim(lax.dynamic_index_in_dim(tile_cols, row_group, 0, keepdims=False), start, TILES_DEV, 0)
    count = tile_counts[row_group, col_group]
    active = jnp.arange(TILES_DEV, dtype=jnp.int32) < count
    return row_group, col_group, plates, row_ids, column_ids, active


def project(tiles, tile_rows, tile_cols, tile_counts, pixels):
    table = rounded(pixels).reshape(SLICES, N_COLS, PT_DEV, TILE)

    def device_term(total, device):
        row_group, col_group, plates, row_ids, column_ids, active = device_slots(tiles, tile_rows, tile_cols, tile_counts, device)
        group = lax.dynamic_index_in_dim(table, col_group, 1, keepdims=False)
        picked = jnp.take(group, column_ids, axis=1)
        product = jnp.einsum('stc,trc->str', picked, plates)
        product = jnp.where(active[None, :, None], product, 0.0)
        part = jnp.zeros((SLICES, RT_DEV, TILE), jnp.float32).at[:, row_ids].add(product)
        return total.at[:, row_group].add(part), None

    total = jnp.zeros((SLICES, N_ROWS, RT_DEV, TILE), jnp.float32)
    total, _ = lax.scan(device_term, total, jnp.arange(N_ROWS * N_COLS, dtype=jnp.int32))
    return total.reshape(SLICES, NRAY)


def backproject(tiles, tile_rows, tile_cols, tile_counts, rays):
    table = rounded(rays).reshape(SLICES, N_ROWS, RT_DEV, TILE)

    def device_term(total, device):
        row_group, col_group, plates, row_ids, column_ids, active = device_slots(tiles, tile_rows, tile_cols, tile_counts, device)
        group = lax.dynamic_index_in_dim(table, row_group, 1, keepdims=False)
        picked = jnp.take(group, row_ids, axis=1)
        product = jnp.einsum('str,trc->stc', picked, plates)
        product = jnp.where(active[None, :, None], product, 0.0)
        part = jnp.zeros((SLICES, PT_DEV, TILE), jnp.float32).at[:, column_ids].add(product)
        return total.at[:, col_group].add(rounded(part)), None

    total = jnp.zeros((SLICES, N_COLS, PT_DEV, TILE), jnp.float32)
    total, _ = lax.scan(device_term, total, jnp.arange(N_ROWS * N_COLS, dtype=jnp.int32))
    return total.reshape(SLICES, NPIX)


def reference(sinogram, tiles, tile_rows, tile_cols, tile_counts):
    residual = sinogram
    gradient = backproject(tiles, tile_rows, tile_cols, tile_counts, residual)
    direction = gradient
    gamma = jnp.sum(gradient * gradient, axis=1)
    solution = jnp.zeros_like(gradient)
    for step_num in range(ITERS):
        image = project(tiles, tile_rows, tile_cols, tile_counts, direction)
        delta = jnp.sum(image * image, axis=1)
        alpha = gamma / (delta + 1e-6)
        solution = solution + alpha[:, None] * direction
        residual = residual - alpha[:, None] * image
        gradient = backproject(tiles, tile_rows, tile_cols, tile_counts, residual)
        if step_num + 1 < ITERS:
            fresh = jnp.sum(gradient * gradient, axis=1)
            direction = gradient + (fresh / (gamma + 1e-6))[:, None] * direction
            gamma = fresh
    return solution, residual, gradient
```

```python
import functools

import jax
import jax.numpy as jnp
from jax import lax
from jax.experimental import pallas as pl
from jax.experimental.pallas import tpu as pltpu
from jax.sharding import PartitionSpec as P

BF, F32 = jnp.bfloat16, jnp.float32
SL = 640
EPS = 1e-6
MESH = pl.DeviceIdType.MESH

def lane(shape):
    return lax.broadcasted_iota(jnp.int32, shape, len(shape) - 1)

def build_w(t_hbm, tv, st, w, sems, chunk=128):
    n = SL // chunk
    def cp(k):
        return pltpu.make_async_copy(t_hbm.at[pl.ds(k * chunk, chunk)], tv.at[k % 2], sems.at[k % 2])
    cp(0).start()
    for k in range(n):
        if k + 1 < n:
            cp(k + 1).start()
        cp(k).wait()
        for q in range(32):
            st[pl.ds(q, chunk, stride=32), :] = tv[k % 2, :, q * 128:(q + 1) * 128].astype(F32)
        @pl.loop(0, chunk // 4)
        def _(b):
            w[k * (chunk // 4) + b] = st[pl.ds(pl.multiple_of(b * 128, 128), 128), :].astype(BF)

def build_oh(rows_v, cols_v, live, ohr, ohc):
    r = rows_v[...]; c = cols_v[...]
    ok = lane((1, SL)) < live
    r = jnp.where(ok, r, -1); c = jnp.where(ok, c, -1)
    @pl.loop(0, 256 // 32)
    def _(i):
        s = lax.broadcasted_iota(jnp.int32, (32, SL), 0) + i * 32
        ohr[pl.ds(pl.multiple_of(i * 32, 32), 32), :] = jnp.where(s == r, 1.0, 0.0).astype(BF)
    @pl.loop(0, 512 // 32)
    def _(i):
        s = lax.broadcasted_iota(jnp.int32, (32, SL), 0) + i * 32
        ohc[pl.ds(pl.multiple_of(i * 32, 32), 32), :] = jnp.where(s == c, 1.0, 0.0).astype(BF)

def rep_mat():
    i = lax.broadcasted_iota(jnp.int32, (128, 512), 0)
    j = lax.broadcasted_iota(jnp.int32, (128, 512), 1)
    return jnp.where(i == (j // 128) * 32 + j % 32, 1.0, 0.0).astype(BF)

def table_b(x, tab):
    e = rep_mat()
    flat = tab.reshape(256 * 16, 128)
    for quad in range(2):
        xs = x[:, :, quad * 128:(quad + 1) * 128].reshape(512, 128)
        y = jnp.dot(xs, e, preferred_element_type=F32)
        for b in range(4):
            s = quad * 4 + b
            yb = y[:, b * 128:(b + 1) * 128].reshape(32, 16, 128)
            for par in range(2):
                flat[pl.ds(par * 8 + s, 256, stride=16), :] = yb[:, par * 8:par * 8 + 8].reshape(256, 128)

def table_a(d, tab):
    low = lane((1, 128)) < 64
    flat = tab.reshape(512 * 16, 128)
    for sp in range(4):
        x = d[:, :, sp * 128:(sp + 1) * 128].reshape(512, 128).astype(F32)
        xr = pltpu.roll(x, 64, 1)
        for s, par, v in ((2 * sp, 0, x), (2 * sp, 1, xr), (2 * sp + 1, 0, xr), (2 * sp + 1, 1, x)):
            v = jnp.where(low, v, 0.0) if par == 0 else jnp.where(low, 0.0, v)
            flat[pl.ds(par * 8 + s, 512, stride=16), :] = v

def main_b(idx, tab, w, p, unroll=20):
    low = lane((8, 128)) < 64
    grp = lane((16, 128)) // 32
    @pl.loop(0, SL // 4 // unroll)
    def _(o):
        lhs, out = [], []
        for u in range(unroll):
            ls = []
            for k in range(4):
                t = idx[0, (o * unroll + u) * 4 + k]
                v = tab[t]
                ls.append(jnp.where(grp == k, v, 0.0).astype(BF))
            lhs.append(jnp.concatenate(ls, 0))
        for u in range(unroll):
            out.append(jnp.dot(lhs[u], w[o * unroll + u], preferred_element_type=F32))
        for u in range(unroll):
            for k in range(4):
                v = jnp.where(low, out[u][16 * k:16 * k + 8], out[u][16 * k + 8:16 * k + 16])
                v = v + pltpu.roll(v, 64, 1)
                p[pl.ds(pl.multiple_of(((o * unroll + u) * 4 + k) * 8, 8), 8), :] = v

def main_a(idx, tab, w, p, unroll=20):
    grp = lane((16, 128)) // 32
    @pl.loop(0, SL // 4 // unroll)
    def _(o):
        lhs, out = [], []
        for u in range(unroll):
            ls = []
            for k in range(4):
                t = idx[0, (o * unroll + u) * 4 + k]
                ls.append(tab[t].astype(BF))
            lhs.append(jnp.concatenate(ls, 0))
        for u in range(unroll):
            out.append(lax.dot_general(lhs[u], w[o * unroll + u], (((1,), (1,)), ((), ())), preferred_element_type=F32))
        for u in range(unroll):
            for k in range(4):
                p[pl.ds(pl.multiple_of(((o * unroll + u) * 4 + k) * 16, 16), 16), :] = jnp.where(grp == k, out[u][16 * k:16 * k + 16], 0.0)

def hilo(m, two):
    hi = m.astype(BF)
    if not two:
        return (hi,)
    return hi, (m - hi.astype(F32)).astype(BF)

def scatter_b(p, ohc, out, two=False):
    low = lane((1, 128)) < 64
    for sp in range(4):
        m = jnp.where(low, p[pl.ds(2 * sp, SL, stride=8), :], p[pl.ds(2 * sp + 1, SL, stride=8), :])
        y = sum(jnp.dot(ohc[...], h, preferred_element_type=F32) for h in hilo(m, two))
        out[:, :, sp * 128:(sp + 1) * 128] = y.astype(BF).reshape(8, 64, 128)

def scatter_a(p, ohr, out, two=False):
    grp = lane((1, 128)) // 32
    for quad in range(2):
        halves = []
        for par in range(2):
            tot = None
            for b in range(4):
                m = p[pl.ds(par * 8 + quad * 4 + b, SL, stride=16), :]
                y = sum(jnp.dot(ohr[...], h, preferred_element_type=F32) for h in hilo(m, two))
                y = y + pltpu.roll(y, 32, 1)
                y = y + pltpu.roll(y, 64, 1)
                tot = y if b == 0 else jnp.where(grp == b, y, tot)
            halves.append(tot.reshape(32, 8, 128))
        out[:, :, quad * 128:(quad + 1) * 128] = jnp.concatenate(halves, 1).astype(BF)


def wait_bytes(buf, n, sem):
    pltpu.make_async_copy(buf.at[pl.ds(0, n)], buf.at[pl.ds(0, n)], sem).wait()


def gather_start(axis, n, buf, send, recv):
    me = lax.axis_index(axis)

    @pl.loop(1, n)
    def _(d):
        to = lax.rem(me + d, n)
        pltpu.make_async_remote_copy(buf.at[me], buf.at[me], send, recv, device_id={axis: to}, device_id_type=MESH).start()


def spread_start(axis, n, parts, buf, send, recv):
    me = lax.axis_index(axis)

    @pl.loop(1, n)
    def _(d):
        to = lax.rem(me + d, n)
        pltpu.make_async_remote_copy(parts.at[to], buf.at[me], send, recv, device_id={axis: to}, device_id_type=MESH).start()

    buf[me] = parts[me]


def group_sums(x, width):
    i = lax.broadcasted_iota(jnp.int32, (256, 8 * width), 0) // 32
    j = lax.broadcasted_iota(jnp.int32, (256, 8 * width), 1) // width
    return jnp.dot(x, jnp.where(i == j, 1.0, 0.0), precision=lax.Precision.HIGHEST, preferred_element_type=F32)


def kernel(nr, nc, rows_s, cols_s, rows_v, cols_v, count, t_hbm, sino, sol_o, res_o, grad_o,
           tv, st, w, ohr, ohc, tb, ta, pb, pa,
           r_all, q0_all, q1_all, rf, g0_all, g1_all, pp0, pp1, pp2, gp0, gp1, gp2, rp0, rp1, qp0, qp1, sc0, sc1,
           g_sh, r_sh, q_sh, sems, tsem):
    i, j = lax.axis_index("rows"), lax.axis_index("cols")
    barrier = pltpu.get_barrier_semaphore()

    @pl.loop(1, nc)
    def _(d):
        pl.semaphore_signal(barrier, inc=1, device_id={"cols": lax.rem(j + d, nc)}, device_id_type=MESH)

    @pl.loop(1, nr)
    def _(d):
        pl.semaphore_signal(barrier, inc=1, device_id={"rows": lax.rem(i + d, nr)}, device_id_type=MESH)

    r_sh[...] = sino[...]
    r_all[j] = sino[...].astype(BF)
    build_oh(rows_v, cols_v, count[0, 0], ohr, ohc)
    pl.semaphore_wait(barrier, nc + nr - 2)
    gather_start("cols", nc, r_all, sems.at[0, 0], sems.at[1, 0])
    build_w(t_hbm, tv, st, w, tsem)
    wait_bytes(r_all, nc - 1, sems.at[1, 0])

    def back(x, parts, buf, ph):
        table_b(x, tb)
        main_b(rows_s, tb, w, pb)
        scatter_b(pb, ohc, parts)
        spread_start("rows", nr, parts, buf, sems.at[0, ph], sems.at[1, ph])
        wait_bytes(buf, nr - 1, sems.at[1, ph])
        return jnp.sum(buf[...].astype(F32), 0)

    def forward(d_all, parts, buf, ph):
        wait_bytes(d_all, nr - 1, sems.at[1, ph])
        table_a(d_all, ta)
        main_a(cols_s, ta, w, pa)
        scatter_a(pa, ohr, parts)
        spread_start("cols", nc, parts, buf, sems.at[0, ph + 1], sems.at[1, ph + 1])
        wait_bytes(buf, nc - 1, sems.at[1, ph + 1])
        return jnp.sum(buf[...].astype(F32), 0)

    def row_sum(v):
        return jnp.sum(v.reshape(-1, 256), 0, keepdims=True)

    def exchange(vals, buf, ph):
        buf[i] = jnp.concatenate(vals + [jnp.zeros((8 - len(vals), 256), F32)], 0)
        gather_start("rows", nr, buf, sems.at[0, ph], sems.at[1, ph])
        wait_bytes(buf, nr - 1, sems.at[1, ph])
        tot = jnp.sum(buf[...], 0)
        return group_sums(tot, 32), group_sums(tot, 64)

    g = back(r_all, pp0, gp0, 1)
    g_sh[...] = g
    g0_all[i] = g.astype(BF)
    gather_start("rows", nr, g0_all, sems.at[0, 2], sems.at[1, 2])
    q = forward(g0_all, rp0, qp0, 2)
    q_sh[...] = q
    q0_all[j] = q.astype(BF)
    gather_start("cols", nc, q0_all, sems.at[0, 4], sems.at[1, 4])
    wait_bytes(q0_all, nc - 1, sems.at[1, 4])
    r0f, q0f = r_all[...].astype(F32), q0_all[...].astype(F32)
    n32, n64 = exchange([row_sum(r0f * q0f), row_sum(q0f * q0f)], sc0, 5)
    alpha = n32[0:1] / (n32[1:2] + EPS)
    alpha_p = n64[0:1] / (n64[1:2] + EPS)
    r1f = r_all[...].astype(F32) - alpha * q0_all[...].astype(F32)
    rf[...] = r1f
    wait_bytes(r_all, nc - 1, sems.at[0, 0])
    r_all[...] = r1f.astype(BF)
    r_sh[...] = r_sh[...] - alpha * q_sh[...]
    sol_o[...] = alpha_p * g_sh[...]
    g1 = back(r_all, pp1, gp1, 6)
    g1_all[i] = g1.astype(BF)
    gather_start("rows", nr, g1_all, sems.at[0, 7], sems.at[1, 7])
    qh = forward(g1_all, rp1, qp1, 7)
    q1_all[j] = qh.astype(BF)
    gather_start("cols", nc, q1_all, sems.at[0, 9], sems.at[1, 9])
    wait_bytes(q1_all, nc - 1, sems.at[1, 9])
    q1f, q0f = q1_all[...].astype(F32), q0_all[...].astype(F32)
    m32, m64 = exchange([row_sum(rf[...] * q1f), row_sum(q1f * q1f), row_sum(q1f * q0f)], sc1, 10)

    def second(n, m):
        beta = m[0:1] / (n[0:1] + EPS)
        delta = m[1:2] + 2.0 * beta * m[2:3] + beta * beta * n[1:2]
        return beta, m[0:1] / (delta + EPS)

    beta, alpha = second(n32, m32)
    beta_p, alpha_p = second(n64, m64)
    r2f = rf[...] - alpha * (q1_all[...].astype(F32) + beta * q0_all[...].astype(F32))
    r_all[...] = r2f.astype(BF)
    res_o[...] = r_sh[...] - alpha * (qh + beta * q_sh[...])
    sol_o[...] = sol_o[...] + alpha_p * (g1 + beta_p * g_sh[...])
    grad_o[...] = back(r_all, pp2, gp2, 11)
    for ph, buf, n in ((1, gp0, nr), (2, g0_all, nr), (3, qp0, nc), (4, q0_all, nc), (5, sc0, nr), (6, gp1, nr),
                       (7, g1_all, nr), (8, qp1, nc), (9, q1_all, nc), (10, sc1, nr), (11, gp2, nr)):
        wait_bytes(buf, n - 1, sems.at[0, ph])


def solution(mesh):
    nr, nc = mesh.shape["rows"], mesh.shape["cols"]

    def body(sinogram, tiles, tile_rows, tile_cols, tile_counts):
        sino = sinogram.reshape(8, 8, 32, 2).transpose(3, 1, 0, 2).reshape(16, 256)
        vm, sm = pl.BlockSpec(memory_space=pltpu.VMEM), pl.BlockSpec(memory_space=pltpu.SMEM)
        ray, pix = (nc, 16, 256), (nr, 64, 512)
        sol, res, grad = pl.pallas_call(
            functools.partial(kernel, nr, nc),
            out_shape=(jax.ShapeDtypeStruct((64, 512), F32), jax.ShapeDtypeStruct((16, 256), F32), jax.ShapeDtypeStruct((64, 512), F32)),
            in_specs=[sm, sm, vm, vm, sm, pl.BlockSpec(memory_space=pl.ANY), vm],
            out_specs=(vm, vm, vm),
            scratch_shapes=[
                pltpu.VMEM((2, 128, 4096), BF), pltpu.VMEM((128 * 32, 128), F32), pltpu.VMEM((160, 128, 128), BF),
                pltpu.VMEM((256, SL), BF), pltpu.VMEM((512, SL), BF), pltpu.VMEM((256, 16, 128), F32), pltpu.VMEM((512, 16, 128), F32),
                pltpu.VMEM((SL * 8, 128), F32), pltpu.VMEM((SL * 16, 128), F32),
                pltpu.VMEM(ray, BF), pltpu.VMEM(ray, BF), pltpu.VMEM(ray, BF), pltpu.VMEM(ray, F32),
                pltpu.VMEM(pix, BF), pltpu.VMEM(pix, BF),
                pltpu.VMEM(pix, BF), pltpu.VMEM(pix, BF), pltpu.VMEM(pix, BF), pltpu.VMEM(pix, BF), pltpu.VMEM(pix, BF), pltpu.VMEM(pix, BF),
                pltpu.VMEM(ray, BF), pltpu.VMEM(ray, BF), pltpu.VMEM(ray, BF), pltpu.VMEM(ray, BF),
                pltpu.VMEM((nr, 8, 256), F32), pltpu.VMEM((nr, 8, 256), F32),
                pltpu.VMEM((64, 512), F32), pltpu.VMEM((16, 256), F32), pltpu.VMEM((16, 256), F32),
                pltpu.SemaphoreType.DMA((2, 12)), pltpu.SemaphoreType.DMA((2,)),
            ],
            compiler_params=pltpu.CompilerParams(collective_id=0, has_side_effects=True, vmem_limit_bytes=60 * 2**20),
            name="cgls",
        )(tile_rows, tile_cols, tile_rows, tile_cols, tile_counts, tiles.reshape(SL, 4096), sino)

        def pixels(x):
            return x.reshape(64, 8, 64).transpose(1, 0, 2).reshape(8, 4096)

        rays = res.reshape(2, 8, 8, 32).transpose(2, 1, 3, 0).reshape(8, 512)
        return pixels(sol), rays, pixels(grad)

    return jax.shard_map(
        body,
        mesh=mesh,
        in_specs=(
            P(None, ("rows", "cols")),
            P("rows", "cols", None),
            P("rows", "cols"),
            P("rows", "cols"),
            P("rows", "cols"),
        ),
        out_specs=(P(None, ("cols", "rows")), P(None, ("rows", "cols")), P(None, ("cols", "rows"))),
        check_vma=False,
    )
```

```python
import functools

import jax
import jax.numpy as jnp
from jax import lax
from jax.experimental import pallas as pl
from jax.experimental.pallas import tpu as pltpu
from jax.sharding import PartitionSpec as P

BF, F32 = jnp.bfloat16, jnp.float32
SL = 640
EPS = 1e-6
MESH = pl.DeviceIdType.MESH
CHUNK = 64
PAD = 40


def lane(shape):
    return lax.broadcasted_iota(jnp.int32, shape, len(shape) - 1)


def sub(shape):
    return lax.broadcasted_iota(jnp.int32, shape, len(shape) - 2)


def tile_copy(t_hbm, tv, sems, k):
    return pltpu.make_async_copy(t_hbm.at[pl.ds(k * CHUNK, CHUNK)], tv.at[k], sems.at[k])


def build_w(tv, st, w, k):
    s = st.at[k % 2]
    for q in range(32):
        s[pl.ds(q, CHUNK, stride=PAD), :] = tv[k, :, q * 128:(q + 1) * 128].astype(F32)
    for b in range(CHUNK // 4):
        w[k * (CHUNK // 4) + b] = jnp.concatenate([s[(b * 4 + m) * PAD:(b * 4 + m) * PAD + 32, :] for m in range(4)], 0).astype(BF)


def build_wt(w, wt, first, end):
    eye = jnp.where(lane((128, 128)) == sub((128, 128)), 1.0, 0.0).astype(BF)

    @pl.loop(first // 20, end // 20)
    def _(o):
        for u in range(20):
            wt[o * 20 + u] = lax.dot_general(eye, w[o * 20 + u], (((1,), (1,)), ((), ())), preferred_element_type=F32).astype(BF)


def build_oh(rows_v, cols_v, live, ohr, ohc):
    at = lane((1, SL))
    perm = jnp.where(sub((SL, SL)) == (at % (SL // 4)) * 4 + at // (SL // 4), 1.0, 0.0).astype(BF)
    ids = jnp.where(at < live, rows_v[...], -1).astype(F32)
    r = jnp.dot(jnp.broadcast_to(ids, (8, SL)).astype(BF), perm, preferred_element_type=F32)[0:1].astype(jnp.int32)
    c = jnp.where(at < live, cols_v[...], -1)

    def fill(oh, n, ids):
        @pl.loop(0, n // 32)
        def _(i):
            s = sub((32, SL)) + i * 32
            oh[pl.ds(pl.multiple_of(i * 32, 32), 32), :] = jnp.where(s == ids, 1.0, 0.0).astype(BF)

    fill(ohr, 256, r)
    fill(ohc, 512, c)


def table_b(x, tab):
    flat = tab.reshape(256 * 8, 128)
    i, j = sub((128, 512)), lane((128, 512))
    e = jnp.where(i == (j // 128) * 32 + j % 32, 1.0, 0.0).astype(BF)
    y = jnp.dot(x[...].reshape(512, 128), e, preferred_element_type=F32)
    for s in range(4):
        ys = y[:, s * 128:(s + 1) * 128].reshape(32, 16, 128)
        for par in range(2):
            flat[pl.ds(par * 4 + s, 256, stride=8), :] = ys[:, par * 8:par * 8 + 8].reshape(256, 128)


def table_a(d, tab):
    flat = tab.reshape(512 * 8, 128)
    for sp in range(2):
        x = d[:, :, sp * 128:(sp + 1) * 128].reshape(512, 128).astype(F32)
        xr = pltpu.roll(x, 64, 1)
        for s, par, v in ((2 * sp, 0, x), (2 * sp, 1, xr), (2 * sp + 1, 0, xr), (2 * sp + 1, 1, x)):
            flat[pl.ds(par * 4 + s, 512, stride=8), :] = v


def main(idx, tab, w, p, forward, unroll):
    grp = lane((8, 128)) // 32
    half = (lane((8, 128)) // 64) == (sub((8, 128)) // 4)

    pad = PAD if forward else 32

    @pl.loop(0, SL // 4 // unroll)
    def _(o):
        lhs, out = [], []
        for u in range(unroll):
            ls = []
            for k in range(4):
                t = idx[0, (o * unroll + u) * 4 + k]
                ls.append(jnp.where(half if forward else grp == k, tab[t], 0.0))
            lhs.append(jnp.concatenate(ls, 0).astype(BF))
        for u in range(unroll):
            out.append(jnp.dot(lhs[u], w[o * unroll + u], preferred_element_type=F32))
        for u in range(unroll):
            p[pl.ds(pl.multiple_of((o * unroll + u) * pad, 8), 32), :] = out[u]


def scatter_b(p, ohc, out):
    low = lane((1, 128)) < 64
    for sp in range(2):
        fs = []
        for s in (2 * sp, 2 * sp + 1):
            m = jnp.where(low, p[pl.ds(s, SL, stride=8), :], p[pl.ds(4 + s, SL, stride=8), :])
            fs.append(m + pltpu.roll(m, 64, 1))
        x = jnp.where(low, fs[0], fs[1]).astype(BF)
        y = jnp.dot(ohc[...], x, preferred_element_type=F32)
        out[:, :, sp * 128:(sp + 1) * 128] = y.astype(BF).reshape(8, 64, 128)


def scatter_a(p, ohr, out):
    grp = lane((1, 128)) // 32
    halves = []
    for par in range(2):
        xs = []
        for k in range(4):
            x = None
            for s in range(4):
                m = p[pl.ds(k * 8 + par * 4 + s, SL // 4, stride=PAD), :]
                if s != k:
                    m = pltpu.roll(m, (32 * (s - k)) % 128, 1)
                x = m if s == 0 else jnp.where(grp == s, m, x)
            xs.append(x.astype(BF))
        y = jnp.dot(ohr[...], jnp.concatenate(xs, 0), preferred_element_type=F32)
        halves.append(y.reshape(32, 8, 128))
    out[...] = jnp.concatenate(halves, 1).astype(BF)


def wait_bytes(buf, n, sem):
    pltpu.make_async_copy(buf.at[pl.ds(0, n)], buf.at[pl.ds(0, n)], sem).wait()


def far_first(a, n):
    return n // 2 + ((a + 1) // 2) * (1 - 2 * (a % 2))


def col_peer(j, m, ny, nz):
    z, y = j // ny, j % ny
    return ((z + far_first(m // ny, nz)) % nz) * ny + (y + far_first(m % ny, ny)) % ny


def row_peer(i, m, nx):
    return ((i // 2 + far_first(m // 2, nx)) % nx) * 2 + (i % 2 + 1 - m % 2) % 2


def expand(x, width):
    e = jnp.where(sub((128, 4 * width)) // 32 == lane((128, 4 * width)) // width, 1.0, 0.0)
    return jnp.dot(x, e, precision=lax.Precision.HIGHEST, preferred_element_type=F32)


def rays_in(x, z, out):
    i, j = sub((128, 512)), lane((128, 512))
    g = j // 128
    e = jnp.where(i == (g // 2) * 64 + (j % 32) * 2 + g % 2, 1.0, 0.0)
    for b in range(4):
        y = jnp.dot(x[:, b * 128:(b + 1) * 128], e, precision=lax.Precision.HIGHEST, preferred_element_type=F32)
        for g in range(4):
            r = (g % 2) * 8 + b * 2 + g // 2
            z[r * 8:r * 8 + 8, :] = y[:, g * 128:(g + 1) * 128]
    grp = lane((1, 128)) // 32
    for h in range(2):
        v = z[pl.ds(h * 4, 16, stride=8), :]
        for s in range(1, 4):
            v = jnp.where(grp == s, z[pl.ds(h * 4 + s, 16, stride=8), :], v)
        out[h] = v


def rays_out(x, z, out):
    grp = lane((1, 128)) // 32
    for h in range(2):
        for s in range(4):
            v = jnp.where(grp == s, x[h], 0.0)
            v = v + pltpu.roll(v, 32, 1)
            z[pl.ds(h * 4 + s, 16, stride=8), :] = v + pltpu.roll(v, 64, 1)
    i, j = sub((128, 128)), lane((128, 128))
    e = jnp.where(i == (j // 64) * 64 + (j % 2) * 32 + (j % 64) // 2, 1.0, 0.0)
    for b in range(4):
        y = None
        for g in range(4):
            r = (g % 2) * 8 + b * 2 + g // 2
            v = z[r * 8:r * 8 + 8, :]
            y = v if g == 0 else jnp.where(grp == g, v, y)
        out[:, b * 128:(b + 1) * 128] = jnp.dot(y, e, precision=lax.Precision.HIGHEST, preferred_element_type=F32)


def pixels_part(x, h, z):
    low = lane((1, 128)) < 64
    for sp in range(2):
        v = x[:, sp * 128:(sp + 1) * 128]
        r = pltpu.roll(v, 64, 1)
        z[pl.ds(h * 4 + 2 * sp, 64, stride=8), :] = jnp.where(low, v, r)
        z[pl.ds(h * 4 + 2 * sp + 1, 64, stride=8), :] = jnp.where(low, r, v)


def pixels_out(z, out):
    low = lane((1, 128)) < 64
    for t in range(32):
        out[:, t * 128:(t + 1) * 128] = jnp.where(low, z[t * 16:t * 16 + 8, :], z[t * 16 + 8:t * 16 + 16, :])


def kernel(nr, nc, ny, rows_s, cols_s, rows_v, cols_v, count, t_hbm, sino, sol_o, res_o, grad_o,
           tv, st, w, wt, ohr, ohc, tb, ta, pb, pa,
           r_all, q0_all, q1_all, rf, g0_all, g1_all, pp, gp, rp, qp, sc,
           g_sh, s_sh, r_sh, q_sh, zr, zs, zg, sems, tsem):
    i, j = lax.axis_index("rows"), lax.axis_index("cols")
    chunks = SL // CHUNK
    for k in range(chunks):
        tile_copy(t_hbm.at[0], tv, tsem, k).start()
    barrier = pltpu.get_barrier_semaphore()

    @pl.loop(0, nc - 1)
    def _(m):
        pl.semaphore_signal(barrier, inc=1, device_id={"cols": col_peer(j, m, ny, nc // ny)}, device_id_type=MESH)

    @pl.loop(0, nr - 1)
    def _(m):
        pl.semaphore_signal(barrier, inc=1, device_id={"rows": row_peer(i, m, nr // 2)}, device_id_type=MESH)

    def to_cols(src, dst, ph, h):
        @pl.loop(0, nc - 1)
        def _(m):
            to = col_peer(j, m, ny, nc // ny)
            pltpu.make_async_remote_copy(src(to), dst.at[j], sems.at[0, ph, h], sems.at[1, ph, h], device_id={"cols": to}, device_id_type=MESH).start()

    def to_rows(src, dst, ph, h):
        @pl.loop(0, nr - 1)
        def _(m):
            to = row_peer(i, m, nr // 2)
            pltpu.make_async_remote_copy(src(to), dst.at[i], sems.at[0, ph, h], sems.at[1, ph, h], device_id={"rows": to}, device_id_type=MESH).start()

    def arrived(buf, n, ph, h):
        wait_bytes(buf, n - 1, sems.at[1, ph, h])

    def left(buf, n, ph, h):
        wait_bytes(buf, n - 1, sems.at[0, ph, h])

    rays_in(sino[...], zr, r_sh)
    for h in range(2):
        r_all[h, j] = r_sh[h].astype(BF)
    build_oh(rows_v, cols_v, count[0, 0], ohr, ohc)
    pl.semaphore_wait(barrier, nc + nr - 2)
    for h in range(2):
        to_cols(lambda to: r_all.at[h, j], r_all.at[h], 0, h)

    for k in range(chunks):
        tile_copy(t_hbm.at[0], tv, tsem, k).wait()

    @pl.loop(0, chunks)
    def _(k):
        build_w(tv, st, w, k)

    def back(h, n, ph):
        table_b(r_all.at[h], tb)
        main(rows_s, tb, w, pb, False, 20)
        parts, buf = pp.at[n, h], gp.at[n, h]
        scatter_b(pb, ohc, parts)
        to_rows(lambda to: parts.at[to], buf, ph, h)
        buf[i] = parts[i]

    def forward(h, n, ph, d_all):
        table_a(d_all, ta)
        main(cols_s, ta, wt, pa, True, 20)
        parts, buf = rp.at[n, h], qp.at[n, h]
        scatter_a(pa, ohr, parts)
        to_cols(lambda to: parts.at[to], buf, ph, h)
        buf[j] = parts[j]

    def total(buf, n, ph, h):
        arrived(buf, n, ph, h)
        return jnp.sum(buf[...].astype(F32), 0)

    def exchange(n, h, vals, ph):
        vals = [jnp.sum(v.reshape(-1, 128), 0, keepdims=True) for v in vals]
        buf = sc.at[n, h]
        buf[i] = jnp.concatenate(vals + [jnp.zeros((8 - len(vals), 128), F32)], 0)
        to_rows(lambda to: buf.at[i], buf, ph, h)

    def exchanged(n, h, ph):
        tot = total(sc.at[n, h], nr, ph, h)
        return expand(tot, 32), expand(tot, 64)

    for h in range(2):
        arrived(r_all.at[h], nc, 0, h)
        back(h, 0, 1)
    build_wt(w, wt, 0, 80)
    for h in range(2):
        g = total(gp.at[0, h], nr, 1, h)
        g_sh[h] = g
        g0_all[h, i] = g.astype(BF)
        to_rows(lambda to: g0_all.at[h, i], g0_all.at[h], 2, h)
    build_wt(w, wt, 80, 160)
    for h in range(2):
        arrived(g0_all.at[h], nr, 2, h)
        forward(h, 0, 3, g0_all.at[h])
    for h in range(2):
        q = total(qp.at[0, h], nc, 3, h)
        q_sh[h] = q
        q0_all[h, j] = q.astype(BF)
        to_cols(lambda to: q0_all.at[h, j], q0_all.at[h], 4, h)
    for h in range(2):
        left(r_all.at[h], nc, 0, h)
        arrived(q0_all.at[h], nc, 4, h)
        r0, q0 = r_all[h].astype(F32), q0_all[h].astype(F32)
        exchange(0, h, [r0 * q0, q0 * q0], 5)
    n32, n64 = [None, None], [None, None]
    for h in range(2):
        n32[h], n64[h] = exchanged(0, h, 5)
        alpha = n32[h][0:1] / (n32[h][1:2] + EPS)
        r1 = r_all[h].astype(F32) - alpha * q0_all[h].astype(F32)
        rf[h] = r1
        r_all[h] = r1.astype(BF)
        back(h, 1, 6)
    for h in range(2):
        alpha, alpha_p = n32[h][0:1] / (n32[h][1:2] + EPS), n64[h][0:1] / (n64[h][1:2] + EPS)
        r_sh[h] = r_sh[h] - alpha * q_sh[h]
        s_sh[h] = alpha_p * g_sh[h]
    for h in range(2):
        g = total(gp.at[1, h], nr, 6, h)
        g1_all[h, i] = g.astype(BF)
        to_rows(lambda to: g1_all.at[h, i], g1_all.at[h], 7, h)
        zg[h] = g
    for h in range(2):
        arrived(g1_all.at[h], nr, 7, h)
        forward(h, 1, 8, g1_all.at[h])
    for h in range(2):
        q = total(qp.at[1, h], nc, 8, h)
        q1_all[h, j] = q.astype(BF)
        to_cols(lambda to: q1_all.at[h, j], q1_all.at[h], 9, h)
        zs[h] = q
    for h in range(2):
        arrived(q1_all.at[h], nc, 9, h)
        q1, q0 = q1_all[h].astype(F32), q0_all[h].astype(F32)
        exchange(1, h, [rf[h] * q1, q1 * q1, q1 * q0], 10)

    def second(n, m):
        beta = m[0:1] / (n[0:1] + EPS)
        delta = m[1:2] + 2.0 * beta * m[2:3] + beta * beta * n[1:2]
        return beta, m[0:1] / (delta + EPS)

    m32, m64 = [None, None], [None, None]
    for h in range(2):
        m32[h], m64[h] = exchanged(1, h, 10)
        beta, alpha = second(n32[h], m32[h])
        r_all[h] = (rf[h] - alpha * (q1_all[h].astype(F32) + beta * q0_all[h].astype(F32))).astype(BF)
        back(h, 2, 11)
    for h in range(2):
        beta, alpha = second(n32[h], m32[h])
        r_sh[h] = r_sh[h] - alpha * (zs[h] + beta * q_sh[h])
        beta, alpha = second(n64[h], m64[h])
        pixels_part(s_sh[h] + alpha * (zg[h] + beta * g_sh[h]), h, zr)
    pixels_out(zr, sol_o)
    rays_out(r_sh, zr, res_o)
    for h in range(2):
        pixels_part(total(gp.at[2, h], nr, 11, h), h, zr)
    pixels_out(zr, grad_o)
    for h in range(2):
        for ph, buf, n in ((1, gp.at[0], nr), (2, g0_all, nr), (3, qp.at[0], nc), (4, q0_all, nc), (5, sc.at[0], nr), (6, gp.at[1], nr),
                           (7, g1_all, nr), (8, qp.at[1], nc), (9, q1_all, nc), (10, sc.at[1], nr), (11, gp.at[2], nr)):
            left(buf.at[h], n, ph, h)


def solution(mesh):
    nr, nc = mesh.shape["rows"], mesh.shape["cols"]
    ny = 4

    def body(sinogram, tiles, tile_rows, tile_cols, tile_counts):
        vm, sm = pl.BlockSpec(memory_space=pltpu.VMEM), pl.BlockSpec(memory_space=pltpu.SMEM)

        def ray(n, t=BF):
            return pltpu.VMEM((*n, nc, 16, 128), t)

        def pix(n):
            return pltpu.VMEM((*n, nr, 64, 256), BF)

        return pl.pallas_call(
            functools.partial(kernel, nr, nc, ny),
            out_shape=(jax.ShapeDtypeStruct((8, 4096), F32), jax.ShapeDtypeStruct((8, 512), F32), jax.ShapeDtypeStruct((8, 4096), F32)),
            in_specs=[sm, sm, vm, vm, sm, pl.BlockSpec(memory_space=pl.ANY), vm],
            out_specs=(vm, vm, vm),
            scratch_shapes=[
                pltpu.VMEM((SL // CHUNK, CHUNK, 4096), BF), pltpu.VMEM((2, CHUNK * PAD, 128), F32),
                pltpu.VMEM((160, 128, 128), BF), pltpu.VMEM((160, 128, 128), BF),
                pltpu.VMEM((256, SL), BF), pltpu.VMEM((512, SL), BF), pltpu.VMEM((256, 8, 128), F32), pltpu.VMEM((512, 8, 128), F32),
                pltpu.VMEM((SL * 8, 128), F32), pltpu.VMEM((160 * PAD, 128), F32),
                ray((2,)), ray((2,)), ray((2,)), ray((2,), F32),
                pix((2,)), pix((2,)), pix((3, 2)), pix((3, 2)), ray((2, 2)), ray((2, 2)), pltpu.VMEM((2, 2, nr, 8, 128), F32),
                pltpu.VMEM((2, 64, 256), F32), pltpu.VMEM((2, 64, 256), F32), pltpu.VMEM((2, 16, 128), F32), pltpu.VMEM((2, 16, 128), F32),
                pltpu.VMEM((512, 128), F32), pltpu.VMEM((2, 16, 128), F32), pltpu.VMEM((2, 64, 256), F32),
                pltpu.SemaphoreType.DMA((2, 12, 2)), pltpu.SemaphoreType.DMA((SL // CHUNK,)),
            ],
            compiler_params=pltpu.CompilerParams(collective_id=0, has_side_effects=True, vmem_limit_bytes=60 * 2**20),
            name="cgls",
        )(tile_rows, tile_cols, tile_rows, tile_cols, tile_counts, tiles, sinogram)

    return jax.shard_map(
        body,
        mesh=mesh,
        in_specs=(
            P(None, ("rows", "cols")),
            P("rows", "cols", None),
            P("rows", "cols"),
            P("rows", "cols"),
            P("rows", "cols"),
        ),
        out_specs=(P(None, ("cols", "rows")), P(None, ("rows", "cols")), P(None, ("cols", "rows"))),
        check_vma=False,
    )
```

```python
import functools

import jax
import jax.numpy as jnp
from jax import lax
from jax.experimental import pallas as pl
from jax.experimental.pallas import tpu as pltpu
from jax.sharding import PartitionSpec as P

BF, F32 = jnp.bfloat16, jnp.float32
SL = 640
EPS = 1e-6
MESH = pl.DeviceIdType.MESH
CHUNK = 64
PAD = 40


def lane(shape):
    return lax.broadcasted_iota(jnp.int32, shape, len(shape) - 1)


def sub(shape):
    return lax.broadcasted_iota(jnp.int32, shape, len(shape) - 2)


def tile_copy(t_hbm, tv, sems, k):
    return pltpu.make_async_copy(t_hbm.at[pl.ds(k * CHUNK, CHUNK)], tv.at[k], sems.at[k])


def build_w(tv, st, w, k):
    s = st.at[k % 2]
    for q in range(32):
        s[pl.ds(q, CHUNK, stride=PAD), :] = tv[k, :, q * 128:(q + 1) * 128].astype(F32)
    for b in range(CHUNK // 4):
        w[k * (CHUNK // 4) + b] = jnp.concatenate([s[(b * 4 + m) * PAD:(b * 4 + m) * PAD + 32, :] for m in range(4)], 0).astype(BF)


def build_wt(w, wt, first, end):
    eye = jnp.where(lane((128, 128)) == sub((128, 128)), 1.0, 0.0).astype(BF)

    @pl.loop(first // 20, end // 20)
    def _(o):
        for u in range(20):
            wt[o * 20 + u] = lax.dot_general(eye, w[o * 20 + u], (((1,), (1,)), ((), ())), preferred_element_type=F32).astype(BF)


def build_oh(rows_v, cols_v, live, ohr, ohc):
    at = lane((1, SL))
    perm = jnp.where(sub((SL, SL)) == (at % (SL // 4)) * 4 + at // (SL // 4), 1.0, 0.0).astype(BF)
    ids = jnp.where(at < live, rows_v[...], -1).astype(F32)
    r = jnp.dot(jnp.broadcast_to(ids, (8, SL)).astype(BF), perm, preferred_element_type=F32)[0:1].astype(jnp.int32)
    c = jnp.where(at < live, cols_v[...], -1)

    def fill(oh, n, ids):
        @pl.loop(0, n // 32)
        def _(i):
            s = sub((32, SL)) + i * 32
            oh[pl.ds(pl.multiple_of(i * 32, 32), 32), :] = jnp.where(s == ids, 1.0, 0.0).astype(BF)

    fill(ohr, 256, r)
    fill(ohc, 512, c)


def table_b(x, tab):
    flat = tab.reshape(256 * 8, 128)
    i, j = sub((128, 512)), lane((128, 512))
    e = jnp.where(i == (j // 128) * 32 + j % 32, 1.0, 0.0).astype(BF)
    y = jnp.dot(x[...].reshape(512, 128), e, preferred_element_type=F32)
    for s in range(4):
        ys = y[:, s * 128:(s + 1) * 128].reshape(32, 16, 128)
        for par in range(2):
            flat[pl.ds(par * 4 + s, 256, stride=8), :] = ys[:, par * 8:par * 8 + 8].reshape(256, 128)


def table_a(d, tab):
    flat = tab.reshape(512 * 8, 128)
    for sp in range(2):
        x = d[:, :, sp * 128:(sp + 1) * 128].reshape(512, 128).astype(F32)
        xr = pltpu.roll(x, 64, 1)
        for s, par, v in ((2 * sp, 0, x), (2 * sp, 1, xr), (2 * sp + 1, 0, xr), (2 * sp + 1, 1, x)):
            flat[pl.ds(par * 4 + s, 512, stride=8), :] = v


def main(idx, tab, w, p, forward, unroll):
    grp = lane((8, 128)) // 32
    half = (lane((8, 128)) // 64) == (sub((8, 128)) // 4)

    pad = PAD if forward else 32

    @pl.loop(0, SL // 4 // unroll)
    def _(o):
        lhs, out = [], []
        for u in range(unroll):
            ls = []
            for k in range(4):
                t = idx[0, (o * unroll + u) * 4 + k]
                ls.append(jnp.where(half if forward else grp == k, tab[t], 0.0))
            lhs.append(jnp.concatenate(ls, 0).astype(BF))
        for u in range(unroll):
            out.append(jnp.dot(lhs[u], w[o * unroll + u], preferred_element_type=F32))
        for u in range(unroll):
            p[pl.ds(pl.multiple_of((o * unroll + u) * pad, 8), 32), :] = out[u]


def scatter_b(p, ohc, emit):
    low = lane((1, 128)) < 64
    for sp in range(2):
        fs = []
        for s in (2 * sp, 2 * sp + 1):
            m = jnp.where(low, p[pl.ds(s, SL, stride=8), :], p[pl.ds(4 + s, SL, stride=8), :])
            fs.append(m + pltpu.roll(m, 64, 1))
        x = jnp.where(low, fs[0], fs[1]).astype(BF)
        emit(sp, jnp.dot(ohc[...], x, preferred_element_type=F32))


def scatter_a(p, ohr, out):
    grp = lane((1, 128)) // 32
    halves = []
    for par in range(2):
        xs = []
        for k in range(4):
            x = None
            for s in range(4):
                m = p[pl.ds(k * 8 + par * 4 + s, SL // 4, stride=PAD), :]
                if s != k:
                    m = pltpu.roll(m, (32 * (s - k)) % 128, 1)
                x = m if s == 0 else jnp.where(grp == s, m, x)
            xs.append(x.astype(BF))
        y = jnp.dot(ohr[...], jnp.concatenate(xs, 0), preferred_element_type=F32)
        halves.append(y.reshape(32, 8, 128))
    out[...] = jnp.concatenate(halves, 1).astype(BF)


def wait_bytes(buf, n, sem):
    pltpu.make_async_copy(buf.at[pl.ds(0, n)], buf.at[pl.ds(0, n)], sem).wait()


def ring(n):
    return sorted(range(n), key=lambda d: -min(d, n - d))


def expand(x, width):
    e = jnp.where(sub((128, 4 * width)) // 32 == lane((128, 4 * width)) // width, 1.0, 0.0)
    return jnp.dot(x, e, precision=lax.Precision.HIGHEST, preferred_element_type=F32)


def rays_in(x, z, out):
    i, j = sub((128, 512)), lane((128, 512))
    g = j // 128
    e = jnp.where(i == (g // 2) * 64 + (j % 32) * 2 + g % 2, 1.0, 0.0)
    for b in range(4):
        y = jnp.dot(x[:, b * 128:(b + 1) * 128], e, precision=lax.Precision.HIGHEST, preferred_element_type=F32)
        for g in range(4):
            r = (g % 2) * 8 + b * 2 + g // 2
            z[r * 8:r * 8 + 8, :] = y[:, g * 128:(g + 1) * 128]
    grp = lane((1, 128)) // 32
    for h in range(2):
        v = z[pl.ds(h * 4, 16, stride=8), :]
        for s in range(1, 4):
            v = jnp.where(grp == s, z[pl.ds(h * 4 + s, 16, stride=8), :], v)
        out[h] = v


def rays_out(x, z, out):
    grp = lane((1, 128)) // 32
    for h in range(2):
        for s in range(4):
            v = jnp.where(grp == s, x[h], 0.0)
            v = v + pltpu.roll(v, 32, 1)
            z[pl.ds(h * 4 + s, 16, stride=8), :] = v + pltpu.roll(v, 64, 1)
    i, j = sub((128, 128)), lane((128, 128))
    e = jnp.where(i == (j // 64) * 64 + (j % 2) * 32 + (j % 64) // 2, 1.0, 0.0)
    for b in range(4):
        y = None
        for g in range(4):
            r = (g % 2) * 8 + b * 2 + g // 2
            v = z[r * 8:r * 8 + 8, :]
            y = v if g == 0 else jnp.where(grp == g, v, y)
        out[:, b * 128:(b + 1) * 128] = jnp.dot(y, e, precision=lax.Precision.HIGHEST, preferred_element_type=F32)


def pixels_part(x, h, z):
    low = lane((1, 128)) < 64
    for sp in range(2):
        v = x[:, sp * 128:(sp + 1) * 128]
        r = pltpu.roll(v, 64, 1)
        z[pl.ds(h * 4 + 2 * sp, 64, stride=8), :] = jnp.where(low, v, r)
        z[pl.ds(h * 4 + 2 * sp + 1, 64, stride=8), :] = jnp.where(low, r, v)


def pixels_out(z, out):
    low = lane((1, 128)) < 64
    for t in range(32):
        out[:, t * 128:(t + 1) * 128] = jnp.where(low, z[t * 16:t * 16 + 8, :], z[t * 16 + 8:t * 16 + 16, :])


def kernel(nr, nc, ny, rows_s, cols_s, rows_v, cols_v, count, t_hbm, sino, sol_o, res_o, grad_o,
           tv, st, w, wt, ohr, ohc, tb, ta, pb, pa,
           r_all, q0_all, q1_all, sr, sq, s1, g0_all, g1_all, pp, gp, rp, qp, sc,
           g_sh, r_sh, q_sh, zr, zs, zg, sems, tsem):
    i, j = lax.axis_index("rows"), lax.axis_index("cols")
    chunks = SL // CHUNK
    for k in range(chunks):
        tile_copy(t_hbm.at[0], tv, tsem, k).start()
    nx, nz = nr // 2, nc // ny
    x, core, z, y = i // 2, lax.rem(i, 2), j // ny, lax.rem(j, ny)
    cols = [lax.rem(z + dz, nz) * ny + lax.rem(y + dy, ny) for dz in ring(nz) for dy in ring(ny)][:-1]
    rows = [lax.rem(x + dx, nx) * 2 + (1 - core if dc else core) for dx in ring(nx) for dc in (1, 0)][:-1]
    barrier = pltpu.get_barrier_semaphore()
    for to in cols:
        pl.semaphore_signal(barrier, inc=1, device_id={"cols": to}, device_id_type=MESH)
    for to in rows:
        pl.semaphore_signal(barrier, inc=1, device_id={"rows": to}, device_id_type=MESH)

    def to_cols(src, dst, ph, h):
        for to in cols:
            pltpu.make_async_remote_copy(src(to), dst.at[j], sems.at[0, ph, h], sems.at[1, ph, h], device_id={"cols": to}, device_id_type=MESH).start()

    def to_rows(src, dst, ph, h):
        for to in rows:
            pltpu.make_async_remote_copy(src(to), dst.at[i], sems.at[0, ph, h], sems.at[1, ph, h], device_id={"rows": to}, device_id_type=MESH).start()

    def arrived(buf, n, ph, h):
        wait_bytes(buf, n - 1, sems.at[1, ph, h])

    def left(buf, n, ph, h):
        wait_bytes(buf, n - 1, sems.at[0, ph, h])

    rays_in(sino[...], zr, r_sh)
    for h in range(2):
        r_all[h, j] = r_sh[h].astype(BF)
    build_oh(rows_v, cols_v, count[0, 0], ohr, ohc)
    pl.semaphore_wait(barrier, nc + nr - 2)
    for h in range(2):
        to_cols(lambda to: r_all.at[h, j], r_all.at[h], 0, h)

    for k in range(chunks):
        tile_copy(t_hbm.at[0], tv, tsem, k).wait()

    @pl.loop(0, chunks)
    def _(k):
        build_w(tv, st, w, k)

    def back(h, src):
        table_b(src.at[h], tb)
        main(rows_s, tb, w, pb, False, 80)

    def sums_of(to):
        def emit(sp, y):
            to[:, sp * 128:(sp + 1) * 128] = y

        scatter_b(pb, ohc, emit)

    def spread(h, n, ph, sums):
        parts, buf = pp.at[n, h], gp.at[n, h]
        parts[...] = sums.astype(BF).reshape(nr, 64, 256)
        to_rows(lambda to: parts.at[to], buf, ph, h)
        buf[i] = parts[i]

    def forward(h, n, ph, d_all):
        table_a(d_all, ta)
        main(cols_s, ta, wt, pa, True, 80)
        parts, buf = rp.at[n, h], qp.at[n, h]
        scatter_a(pa, ohr, parts)
        to_cols(lambda to: parts.at[to], buf, ph, h)
        buf[j] = parts[j]

    def total(buf, n, ph, h):
        arrived(buf, n, ph, h)
        return jnp.sum(buf[...].astype(F32), 0)

    def exchange(n, h, vals, ph):
        vals = [jnp.sum(v.reshape(-1, 128), 0, keepdims=True) for v in vals]
        buf = sc.at[n, h]
        buf[i] = jnp.concatenate(vals + [jnp.zeros((8 - len(vals), 128), F32)], 0)
        to_rows(lambda to: buf.at[i], buf, ph, h)

    def exchanged(n, h, ph):
        tot = total(sc.at[n, h], nr, ph, h)
        return expand(tot, 32), expand(tot, 64)

    for h in range(2):
        arrived(r_all.at[h], nc, 0, h)
        back(h, r_all)
        sums_of(sr.at[h])
        spread(h, 0, 1, sr[h])
    build_wt(w, wt, 0, 80)
    for h in range(2):
        g = total(gp.at[0, h], nr, 1, h)
        g0_all[h, i] = g.astype(BF)
        to_rows(lambda to: g0_all.at[h, i], g0_all.at[h], 2, h)
        g_sh[h] = g
    build_wt(w, wt, 80, 160)
    for h in range(2):
        arrived(g0_all.at[h], nr, 2, h)
        forward(h, 0, 3, g0_all.at[h])
    for h in range(2):
        q = total(qp.at[0, h], nc, 3, h)
        q0_all[h, j] = q.astype(BF)
        to_cols(lambda to: q0_all.at[h, j], q0_all.at[h], 4, h)
        q_sh[h] = q
    n32, n64 = [None, None], [None, None]

    def norms0(h):
        arrived(q0_all.at[h], nc, 4, h)
        r0, q0 = r_all[h].astype(F32), q0_all[h].astype(F32)
        exchange(0, h, [r0 * q0, q0 * q0], 5)

    def step0(h):
        n32[h], n64[h] = exchanged(0, h, 5)
        v = sr[h] - n64[h][0:1] / (n64[h][1:2] + EPS) * sq[h]
        spread(h, 1, 6, v)
        sr[h] = v

    norms0(0)
    back(0, q0_all)
    sums_of(sq.at[0])
    norms0(1)
    step0(0)
    back(1, q0_all)
    sums_of(sq.at[1])
    step0(1)
    for h in range(2):
        r_sh[h] = r_sh[h] - n32[h][0:1] / (n32[h][1:2] + EPS) * q_sh[h]
    for h in range(2):
        g = total(gp.at[1, h], nr, 6, h)
        g1_all[h, i] = g.astype(BF)
        to_rows(lambda to: g1_all.at[h, i], g1_all.at[h], 7, h)
        zg[h] = g
    for h in range(2):
        arrived(g1_all.at[h], nr, 7, h)
        forward(h, 1, 8, g1_all.at[h])
    for h in range(2):
        q = total(qp.at[1, h], nc, 8, h)
        q1_all[h, j] = q.astype(BF)
        to_cols(lambda to: q1_all.at[h, j], q1_all.at[h], 9, h)
        zs[h] = q

    def norms1(h):
        arrived(q1_all.at[h], nc, 9, h)
        r0, q0, q1 = r_all[h].astype(F32), q0_all[h].astype(F32), q1_all[h].astype(F32)
        exchange(1, h, [r0 * q1, q1 * q1, q1 * q0], 10)

    def scalars(n, m):
        alpha = n[0:1] / (n[1:2] + EPS)
        gamma = m[0:1] - alpha * m[2:3]
        beta = gamma / (n[0:1] + EPS)
        delta = m[1:2] + 2.0 * beta * m[2:3] + beta * beta * n[1:2]
        return alpha, beta, gamma / (delta + EPS)

    m32, m64 = [None, None], [None, None]

    def step1(h):
        m32[h], m64[h] = exchanged(1, h, 10)
        _, beta, alpha = scalars(n64[h], m64[h])
        spread(h, 2, 11, sr[h] - alpha * (s1[...] + beta * sq[h]))

    norms1(0)
    back(0, q1_all)
    sums_of(s1)
    norms1(1)
    step1(0)
    back(1, q1_all)
    sums_of(s1)
    step1(1)
    for h in range(2):
        _, beta, alpha = scalars(n32[h], m32[h])
        r_sh[h] = r_sh[h] - alpha * (zs[h] + beta * q_sh[h])
        alpha0, beta, alpha = scalars(n64[h], m64[h])
        pixels_part(alpha0 * g_sh[h] + alpha * (zg[h] + beta * g_sh[h]), h, zr)
    pixels_out(zr, sol_o)
    rays_out(r_sh, zr, res_o)
    for h in range(2):
        pixels_part(total(gp.at[2, h], nr, 11, h), h, zr)
    pixels_out(zr, grad_o)
    for h in range(2):
        for ph, buf, n in ((0, r_all, nc), (1, gp.at[0], nr), (2, g0_all, nr), (3, qp.at[0], nc), (4, q0_all, nc), (5, sc.at[0], nr), (6, gp.at[1], nr),
                           (7, g1_all, nr), (8, qp.at[1], nc), (9, q1_all, nc), (10, sc.at[1], nr), (11, gp.at[2], nr)):
            left(buf.at[h], n, ph, h)


def write(a, b, c, x, y, z):
    x[...] = a[...]
    y[...] = b[...]
    z[...] = c[...]


def solution(mesh):
    nr, nc = mesh.shape["rows"], mesh.shape["cols"]
    ny = 4

    def body(sinogram, tiles, tile_rows, tile_cols, tile_counts):
        vm, sm = pl.BlockSpec(memory_space=pltpu.VMEM), pl.BlockSpec(memory_space=pltpu.SMEM)

        def ray(n, t=BF):
            return pltpu.VMEM((*n, nc, 16, 128), t)

        def pix(n):
            return pltpu.VMEM((*n, nr, 64, 256), BF)

        outs = (jax.ShapeDtypeStruct((8, 4096), F32), jax.ShapeDtypeStruct((8, 512), F32), jax.ShapeDtypeStruct((8, 4096), F32))
        made = pl.pallas_call(
            functools.partial(kernel, nr, nc, ny),
            out_shape=outs,
            in_specs=[sm, sm, vm, vm, sm, pl.BlockSpec(memory_space=pl.ANY), vm],
            out_specs=(vm, vm, vm),
            scratch_shapes=[
                pltpu.VMEM((SL // CHUNK, CHUNK, 4096), BF), pltpu.VMEM((2, CHUNK * PAD, 128), F32),
                pltpu.VMEM((160, 128, 128), BF), pltpu.VMEM((160, 128, 128), BF),
                pltpu.VMEM((256, SL), BF), pltpu.VMEM((512, SL), BF), pltpu.VMEM((256, 8, 128), F32), pltpu.VMEM((512, 8, 128), F32),
                pltpu.VMEM((SL * 8, 128), F32), pltpu.VMEM((160 * PAD, 128), F32),
                ray((2,)), ray((2,)), ray((2,)), pltpu.VMEM((2, 512, 256), F32), pltpu.VMEM((2, 512, 256), F32), pltpu.VMEM((512, 256), F32),
                pix((2,)), pix((2,)), pix((3, 2)), pix((3, 2)), ray((2, 2)), ray((2, 2)), pltpu.VMEM((2, 2, nr, 8, 128), F32),
                pltpu.VMEM((2, 64, 256), F32), pltpu.VMEM((2, 16, 128), F32), pltpu.VMEM((2, 16, 128), F32),
                pltpu.VMEM((512, 128), F32), pltpu.VMEM((2, 16, 128), F32), pltpu.VMEM((2, 64, 256), F32),
                pltpu.SemaphoreType.DMA((2, 12, 2)), pltpu.SemaphoreType.DMA((SL // CHUNK,)),
            ],
            compiler_params=pltpu.CompilerParams(collective_id=0, has_side_effects=True, vmem_limit_bytes=60 * 2**20),
            name="cgls",
        )(tile_rows, tile_cols, tile_rows, tile_cols, tile_counts, tiles, sinogram)
        return pl.pallas_call(
            write,
            out_shape=outs,
            in_specs=[vm] * 3,
            out_specs=(vm,) * 3,
            name="write",
        )(*made)

    return jax.shard_map(
        body,
        mesh=mesh,
        in_specs=(
            P(None, ("rows", "cols")),
            P("rows", "cols", None),
            P("rows", "cols"),
            P("rows", "cols"),
            P("rows", "cols"),
        ),
        out_specs=(P(None, ("cols", "rows")), P(None, ("rows", "cols")), P(None, ("cols", "rows"))),
        check_vma=False,
    )
```

```python
import functools

import jax
import jax.numpy as jnp
from jax import lax
from jax.experimental import pallas as pl
from jax.experimental.pallas import tpu as pltpu
from jax.sharding import PartitionSpec as P

BF, F32 = jnp.bfloat16, jnp.float32
SL = 640
EPS = 1e-6
MESH = pl.DeviceIdType.MESH
CHUNK = 64
PAD = 40


def lane(shape):
    return lax.broadcasted_iota(jnp.int32, shape, len(shape) - 1)


def sub(shape):
    return lax.broadcasted_iota(jnp.int32, shape, len(shape) - 2)


def tile_copy(t_hbm, tv, sems, k):
    return pltpu.make_async_copy(t_hbm.at[pl.ds(k * CHUNK, CHUNK)], tv.at[k], sems.at[k])


def build_w(tv, st, w, k):
    s = st.at[k % 2]
    for q in range(32):
        s[pl.ds(q, CHUNK, stride=PAD), :] = tv[k, :, q * 128:(q + 1) * 128].astype(F32)
    for b in range(CHUNK // 4):
        w[k * (CHUNK // 4) + b] = jnp.concatenate([s[(b * 4 + m) * PAD:(b * 4 + m) * PAD + 32, :] for m in range(4)], 0).astype(BF)


def build_wt(w, wt, first, end):
    eye = jnp.where(lane((128, 128)) == sub((128, 128)), 1.0, 0.0).astype(BF)

    @pl.loop(first // 20, end // 20)
    def _(o):
        for u in range(20):
            wt[o * 20 + u] = lax.dot_general(eye, w[o * 20 + u], (((1,), (1,)), ((), ())), preferred_element_type=F32).astype(BF)


def build_oh(rows_v, cols_v, live, ohr, ohc):
    at = lane((1, SL))
    perm = jnp.where(sub((SL, SL)) == (at % (SL // 4)) * 4 + at // (SL // 4), 1.0, 0.0).astype(BF)
    ids = jnp.where(at < live, rows_v[...], -1).astype(F32)
    r = jnp.dot(jnp.broadcast_to(ids, (8, SL)).astype(BF), perm, preferred_element_type=F32)[0:1].astype(jnp.int32)
    c = jnp.where(at < live, cols_v[...], -1)

    def fill(oh, n, ids):
        @pl.loop(0, n // 32)
        def _(i):
            s = sub((32, SL)) + i * 32
            oh[pl.ds(pl.multiple_of(i * 32, 32), 32), :] = jnp.where(s == ids, 1.0, 0.0).astype(BF)

    fill(ohr, 256, r)
    fill(ohc, 512, c)


def table_b(x, tab):
    flat = tab.reshape(256 * 8, 128)
    i, j = sub((128, 512)), lane((128, 512))
    e = jnp.where(i == (j // 128) * 32 + j % 32, 1.0, 0.0).astype(BF)
    y = jnp.dot(x[...].reshape(512, 128), e, preferred_element_type=F32)
    for s in range(4):
        ys = y[:, s * 128:(s + 1) * 128].reshape(32, 16, 128)
        for par in range(2):
            flat[pl.ds(par * 4 + s, 256, stride=8), :] = ys[:, par * 8:par * 8 + 8].reshape(256, 128)


def table_a(d, tab):
    flat = tab.reshape(512 * 8, 128)
    for sp in range(2):
        x = d[:, :, sp * 128:(sp + 1) * 128].reshape(512, 128).astype(F32)
        xr = pltpu.roll(x, 64, 1)
        for s, par, v in ((2 * sp, 0, x), (2 * sp, 1, xr), (2 * sp + 1, 0, xr), (2 * sp + 1, 1, x)):
            flat[pl.ds(par * 4 + s, 512, stride=8), :] = v


def main(idx, tab, w, p, forward, unroll):
    grp = lane((8, 128)) // 32
    half = (lane((8, 128)) // 64) == (sub((8, 128)) // 4)

    pad = PAD if forward else 32
    zero = jnp.zeros((32, 128), BF)

    @pl.loop(0, SL // 8 // unroll)
    def _(o):
        lhs, out = [], []
        for u in range(unroll):
            ls = []
            for g in range(2):
                rs = []
                for k in range(4):
                    t = idx[0, (o * unroll + u) * 8 + g * 4 + k]
                    rs.append(jnp.where(half if forward else grp == k, tab[t], 0.0))
                v = jnp.concatenate(rs, 0).astype(BF)
                ls.append(jnp.concatenate([zero, v] if g else [v, zero], 1))
            lhs.append(jnp.concatenate(ls, 0))
        for u in range(unroll):
            rhs = w[pl.ds((o * unroll + u) * 2, 2)].reshape(256, 128)
            out.append(jnp.dot(lhs[u], rhs, preferred_element_type=F32))
        for u in range(unroll):
            for g in range(2):
                p[pl.ds(pl.multiple_of(((o * unroll + u) * 2 + g) * pad, 8), 32), :] = out[u][g * 32:g * 32 + 32]


def scatter_b(p, ohc, emit):
    low = lane((1, 128)) < 64
    for sp in range(2):
        fs = []
        for s in (2 * sp, 2 * sp + 1):
            m = jnp.where(low, p[pl.ds(s, SL, stride=8), :], p[pl.ds(4 + s, SL, stride=8), :])
            fs.append(m + pltpu.roll(m, 64, 1))
        x = jnp.where(low, fs[0], fs[1]).astype(BF)
        emit(sp, jnp.dot(ohc[...], x, preferred_element_type=F32))


def scatter_a(p, ohr, out):
    grp = lane((1, 128)) // 32
    halves = []
    for par in range(2):
        xs = []
        for k in range(4):
            x = None
            for s in range(4):
                m = p[pl.ds(k * 8 + par * 4 + s, SL // 4, stride=PAD), :]
                if s != k:
                    m = pltpu.roll(m, (32 * (s - k)) % 128, 1)
                x = m if s == 0 else jnp.where(grp == s, m, x)
            xs.append(x.astype(BF))
        y = jnp.dot(ohr[...], jnp.concatenate(xs, 0), preferred_element_type=F32)
        halves.append(y.reshape(32, 8, 128))
    out[...] = jnp.concatenate(halves, 1).astype(BF)


def wait_bytes(buf, n, sem):
    pltpu.make_async_copy(buf.at[pl.ds(0, n)], buf.at[pl.ds(0, n)], sem).wait()


def ring(n):
    return sorted(range(n), key=lambda d: -min(d, n - d))


def expand(x, width):
    e = jnp.where(sub((128, 4 * width)) // 32 == lane((128, 4 * width)) // width, 1.0, 0.0)
    return jnp.dot(x, e, precision=lax.Precision.HIGHEST, preferred_element_type=F32)


def rays_in(x, z, out):
    i, j = sub((128, 512)), lane((128, 512))
    g = j // 128
    e = jnp.where(i == (g // 2) * 64 + (j % 32) * 2 + g % 2, 1.0, 0.0)
    for b in range(4):
        y = jnp.dot(x[:, b * 128:(b + 1) * 128], e, precision=lax.Precision.HIGHEST, preferred_element_type=F32)
        for g in range(4):
            r = (g % 2) * 8 + b * 2 + g // 2
            z[r * 8:r * 8 + 8, :] = y[:, g * 128:(g + 1) * 128]
    grp = lane((1, 128)) // 32
    for h in range(2):
        v = z[pl.ds(h * 4, 16, stride=8), :]
        for s in range(1, 4):
            v = jnp.where(grp == s, z[pl.ds(h * 4 + s, 16, stride=8), :], v)
        out[h] = v


def rays_out(x, z, out):
    grp = lane((1, 128)) // 32
    for h in range(2):
        for s in range(4):
            v = jnp.where(grp == s, x[h], 0.0)
            v = v + pltpu.roll(v, 32, 1)
            z[pl.ds(h * 4 + s, 16, stride=8), :] = v + pltpu.roll(v, 64, 1)
    i, j = sub((128, 128)), lane((128, 128))
    e = jnp.where(i == (j // 64) * 64 + (j % 2) * 32 + (j % 64) // 2, 1.0, 0.0)
    for b in range(4):
        y = None
        for g in range(4):
            r = (g % 2) * 8 + b * 2 + g // 2
            v = z[r * 8:r * 8 + 8, :]
            y = v if g == 0 else jnp.where(grp == g, v, y)
        out[:, b * 128:(b + 1) * 128] = jnp.dot(y, e, precision=lax.Precision.HIGHEST, preferred_element_type=F32)


def pixels_part(x, h, z):
    low = lane((1, 128)) < 64
    for sp in range(2):
        v = x[:, sp * 128:(sp + 1) * 128]
        r = pltpu.roll(v, 64, 1)
        z[pl.ds(h * 4 + 2 * sp, 64, stride=8), :] = jnp.where(low, v, r)
        z[pl.ds(h * 4 + 2 * sp + 1, 64, stride=8), :] = jnp.where(low, r, v)


def pixels_out(z, out):
    low = lane((1, 128)) < 64
    for t in range(32):
        out[:, t * 128:(t + 1) * 128] = jnp.where(low, z[t * 16:t * 16 + 8, :], z[t * 16 + 8:t * 16 + 16, :])


def kernel(nr, nc, ny, rows_s, cols_s, rows_v, cols_v, count, t_hbm, sino, sol_o, res_o, grad_o,
           tv, st, w, wt, ohr, ohc, tb, ta, pb, pa,
           r_all, q0_all, q1_all, sr, sq, s1, g0_all, g1_all, pp, gp, rp, qp, sc,
           g_sh, r_sh, q_sh, zr, zs, zg, sems, tsem):
    i, j = lax.axis_index("rows"), lax.axis_index("cols")
    chunks = SL // CHUNK
    for k in range(chunks):
        tile_copy(t_hbm.at[0], tv, tsem, k).start()
    nx, nz = nr // 2, nc // ny
    x, core, z, y = i // 2, lax.rem(i, 2), j // ny, lax.rem(j, ny)
    cols = [lax.rem(z + dz, nz) * ny + lax.rem(y + dy, ny) for dz in ring(nz) for dy in ring(ny)][:-1]
    rows = [lax.rem(x + dx, nx) * 2 + (1 - core if dc else core) for dx in ring(nx) for dc in (1, 0)][:-1]
    barrier = pltpu.get_barrier_semaphore()
    for to in cols:
        pl.semaphore_signal(barrier, inc=1, device_id={"cols": to}, device_id_type=MESH)
    for to in rows:
        pl.semaphore_signal(barrier, inc=1, device_id={"rows": to}, device_id_type=MESH)

    def to_cols(src, dst, ph, h):
        for to in cols:
            pltpu.make_async_remote_copy(src(to), dst.at[j], sems.at[0, ph, h], sems.at[1, ph, h], device_id={"cols": to}, device_id_type=MESH).start()

    def to_rows(src, dst, ph, h):
        for to in rows:
            pltpu.make_async_remote_copy(src(to), dst.at[i], sems.at[0, ph, h], sems.at[1, ph, h], device_id={"rows": to}, device_id_type=MESH).start()

    def arrived(buf, n, ph, h):
        wait_bytes(buf, n - 1, sems.at[1, ph, h])

    def left(buf, n, ph, h):
        wait_bytes(buf, n - 1, sems.at[0, ph, h])

    rays_in(sino[...], zr, r_sh)
    for h in range(2):
        r_all[h, j] = r_sh[h].astype(BF)
    build_oh(rows_v, cols_v, count[0, 0], ohr, ohc)
    pl.semaphore_wait(barrier, nc + nr - 2)
    for h in range(2):
        to_cols(lambda to: r_all.at[h, j], r_all.at[h], 0, h)

    for k in range(chunks):
        tile_copy(t_hbm.at[0], tv, tsem, k).wait()

    @pl.loop(0, chunks)
    def _(k):
        build_w(tv, st, w, k)

    def back(h, src):
        table_b(src.at[h], tb)
        main(rows_s, tb, w, pb, False, 20)

    def sums_of(to):
        def emit(sp, y):
            to[:, sp * 128:(sp + 1) * 128] = y

        scatter_b(pb, ohc, emit)

    def spread(h, n, ph, sums):
        parts, buf = pp.at[n, h], gp.at[n, h]
        parts[...] = sums.astype(BF).reshape(nr, 64, 256)
        to_rows(lambda to: parts.at[to], buf, ph, h)
        buf[i] = parts[i]

    def forward(h, n, ph, d_all):
        table_a(d_all, ta)
        main(cols_s, ta, wt, pa, True, 20)
        parts, buf = rp.at[n, h], qp.at[n, h]
        scatter_a(pa, ohr, parts)
        to_cols(lambda to: parts.at[to], buf, ph, h)
        buf[j] = parts[j]

    def total(buf, n, ph, h):
        arrived(buf, n, ph, h)
        return jnp.sum(buf[...].astype(F32), 0)

    def exchange(n, h, vals, ph):
        vals = [jnp.sum(v.reshape(-1, 128), 0, keepdims=True) for v in vals]
        buf = sc.at[n, h]
        buf[i] = jnp.concatenate(vals + [jnp.zeros((8 - len(vals), 128), F32)], 0)
        to_rows(lambda to: buf.at[i], buf, ph, h)

    def exchanged(n, h, ph):
        tot = total(sc.at[n, h], nr, ph, h)
        return expand(tot, 32), expand(tot, 64)

    @pl.loop(0, 2)
    def _(h):
        arrived(r_all.at[h], nc, 0, h)
        back(h, r_all)
        sums_of(sr.at[h])
        spread(h, 0, 1, sr[h])
    build_wt(w, wt, 0, 80)
    for h in range(2):
        g = total(gp.at[0, h], nr, 1, h)
        g0_all[h, i] = g.astype(BF)
        to_rows(lambda to: g0_all.at[h, i], g0_all.at[h], 2, h)
        g_sh[h] = g
    build_wt(w, wt, 80, 160)
    @pl.loop(0, 2)
    def _(h):
        arrived(g0_all.at[h], nr, 2, h)
        forward(h, 0, 3, g0_all.at[h])
    for h in range(2):
        q = total(qp.at[0, h], nc, 3, h)
        q0_all[h, j] = q.astype(BF)
        to_cols(lambda to: q0_all.at[h, j], q0_all.at[h], 4, h)
        q_sh[h] = q
    n32, n64 = [None, None], [None, None]

    def norms0(h):
        arrived(q0_all.at[h], nc, 4, h)
        r0, q0 = r_all[h].astype(F32), q0_all[h].astype(F32)
        exchange(0, h, [r0 * q0, q0 * q0], 5)

    def step0(h):
        n32[h], n64[h] = exchanged(0, h, 5)
        v = sr[h] - n64[h][0:1] / (n64[h][1:2] + EPS) * sq[h]
        spread(h, 1, 6, v)
        sr[h] = v

    norms0(0)
    back(0, q0_all)
    sums_of(sq.at[0])
    norms0(1)
    step0(0)
    back(1, q0_all)
    sums_of(sq.at[1])
    step0(1)
    for h in range(2):
        r_sh[h] = r_sh[h] - n32[h][0:1] / (n32[h][1:2] + EPS) * q_sh[h]
    for h in range(2):
        g = total(gp.at[1, h], nr, 6, h)
        g1_all[h, i] = g.astype(BF)
        to_rows(lambda to: g1_all.at[h, i], g1_all.at[h], 7, h)
        zg[h] = g
    @pl.loop(0, 2)
    def _(h):
        arrived(g1_all.at[h], nr, 7, h)
        forward(h, 1, 8, g1_all.at[h])
    for h in range(2):
        q = total(qp.at[1, h], nc, 8, h)
        q1_all[h, j] = q.astype(BF)
        to_cols(lambda to: q1_all.at[h, j], q1_all.at[h], 9, h)
        zs[h] = q

    def norms1(h):
        arrived(q1_all.at[h], nc, 9, h)
        r0, q0, q1 = r_all[h].astype(F32), q0_all[h].astype(F32), q1_all[h].astype(F32)
        exchange(1, h, [r0 * q1, q1 * q1, q1 * q0], 10)

    def scalars(n, m):
        alpha = n[0:1] / (n[1:2] + EPS)
        gamma = m[0:1] - alpha * m[2:3]
        beta = gamma / (n[0:1] + EPS)
        delta = m[1:2] + 2.0 * beta * m[2:3] + beta * beta * n[1:2]
        return alpha, beta, gamma / (delta + EPS)

    m32, m64 = [None, None], [None, None]

    def step1(h):
        m32[h], m64[h] = exchanged(1, h, 10)
        _, beta, alpha = scalars(n64[h], m64[h])
        spread(h, 2, 11, sr[h] - alpha * (s1[...] + beta * sq[h]))

    norms1(0)
    back(0, q1_all)
    sums_of(s1)
    norms1(1)
    step1(0)
    back(1, q1_all)
    sums_of(s1)
    step1(1)
    for h in range(2):
        _, beta, alpha = scalars(n32[h], m32[h])
        r_sh[h] = r_sh[h] - alpha * (zs[h] + beta * q_sh[h])
        alpha0, beta, alpha = scalars(n64[h], m64[h])
        pixels_part(alpha0 * g_sh[h] + alpha * (zg[h] + beta * g_sh[h]), h, zr)
    pixels_out(zr, sol_o)
    rays_out(r_sh, zr, res_o)
    for h in range(2):
        pixels_part(total(gp.at[2, h], nr, 11, h), h, zr)
    pixels_out(zr, grad_o)
    for h in range(2):
        for ph, buf, n in ((0, r_all, nc), (1, gp.at[0], nr), (2, g0_all, nr), (3, qp.at[0], nc), (4, q0_all, nc), (5, sc.at[0], nr), (6, gp.at[1], nr),
                           (7, g1_all, nr), (8, qp.at[1], nc), (9, q1_all, nc), (10, sc.at[1], nr), (11, gp.at[2], nr)):
            left(buf.at[h], n, ph, h)


def write(a, b, c, x, y, z):
    x[...] = a[...]
    y[...] = b[...]
    z[...] = c[...]


def solution(mesh):
    nr, nc = mesh.shape["rows"], mesh.shape["cols"]
    ny = 4

    def body(sinogram, tiles, tile_rows, tile_cols, tile_counts):
        vm, sm = pl.BlockSpec(memory_space=pltpu.VMEM), pl.BlockSpec(memory_space=pltpu.SMEM)

        def ray(n, t=BF):
            return pltpu.VMEM((*n, nc, 16, 128), t)

        def pix(n):
            return pltpu.VMEM((*n, nr, 64, 256), BF)

        outs = (jax.ShapeDtypeStruct((8, 4096), F32), jax.ShapeDtypeStruct((8, 512), F32), jax.ShapeDtypeStruct((8, 4096), F32))
        made = pl.pallas_call(
            functools.partial(kernel, nr, nc, ny),
            out_shape=outs,
            in_specs=[sm, sm, vm, vm, sm, pl.BlockSpec(memory_space=pl.ANY), vm],
            out_specs=(vm, vm, vm),
            scratch_shapes=[
                pltpu.VMEM((SL // CHUNK, CHUNK, 4096), BF), pltpu.VMEM((2, CHUNK * PAD, 128), F32),
                pltpu.VMEM((160, 128, 128), BF), pltpu.VMEM((160, 128, 128), BF),
                pltpu.VMEM((256, SL), BF), pltpu.VMEM((512, SL), BF), pltpu.VMEM((256, 8, 128), F32), pltpu.VMEM((512, 8, 128), F32),
                pltpu.VMEM((SL * 8, 128), F32), pltpu.VMEM((160 * PAD, 128), F32),
                ray((2,)), ray((2,)), ray((2,)), pltpu.VMEM((2, 512, 256), F32), pltpu.VMEM((2, 512, 256), F32), pltpu.VMEM((512, 256), F32),
                pix((2,)), pix((2,)), pix((3, 2)), pix((3, 2)), ray((2, 2)), ray((2, 2)), pltpu.VMEM((2, 2, nr, 8, 128), F32),
                pltpu.VMEM((2, 64, 256), F32), pltpu.VMEM((2, 16, 128), F32), pltpu.VMEM((2, 16, 128), F32),
                pltpu.VMEM((512, 128), F32), pltpu.VMEM((2, 16, 128), F32), pltpu.VMEM((2, 64, 256), F32),
                pltpu.SemaphoreType.DMA((2, 12, 2)), pltpu.SemaphoreType.DMA((SL // CHUNK,)),
            ],
            compiler_params=pltpu.CompilerParams(collective_id=0, has_side_effects=True, vmem_limit_bytes=60 * 2**20),
            name="cgls",
        )(tile_rows, tile_cols, tile_rows, tile_cols, tile_counts, tiles, sinogram)
        return pl.pallas_call(
            write,
            out_shape=outs,
            in_specs=[vm] * 3,
            out_specs=(vm,) * 3,
            name="write",
        )(*made)

    return jax.shard_map(
        body,
        mesh=mesh,
        in_specs=(
            P(None, ("rows", "cols")),
            P("rows", "cols", None),
            P("rows", "cols"),
            P("rows", "cols"),
            P("rows", "cols"),
        ),
        out_specs=(P(None, ("cols", "rows")), P(None, ("rows", "cols")), P(None, ("cols", "rows"))),
        check_vma=False,
    )
```

```python
import functools

import jax
import jax.numpy as jnp
from jax import lax
from jax.experimental import pallas as pl
from jax.experimental.pallas import tpu as pltpu
from jax.sharding import PartitionSpec as P

BF, F32 = jnp.bfloat16, jnp.float32
SL = 640
EPS = 1e-6
MESH = pl.DeviceIdType.MESH
CHUNK = 64
PAD = 40


def lane(shape):
    return lax.broadcasted_iota(jnp.int32, shape, len(shape) - 1)


def sub(shape):
    return lax.broadcasted_iota(jnp.int32, shape, len(shape) - 2)


def tile_copy(t_hbm, tv, sems, k):
    return pltpu.make_async_copy(t_hbm.at[pl.ds(k * CHUNK, CHUNK)], tv.at[k], sems.at[k])


def build_w(tv, st, w, k):
    s = st.at[k % 2]
    for q in range(32):
        s[pl.ds(q, CHUNK, stride=PAD), :] = tv[k, :, q * 128:(q + 1) * 128].astype(F32)
    for b in range(CHUNK // 4):
        w[k * (CHUNK // 4) + b] = jnp.concatenate([s[(b * 4 + m) * PAD:(b * 4 + m) * PAD + 32, :] for m in range(4)], 0).astype(BF)


def build_wt(w, wt, first, end):
    eye = jnp.where(lane((128, 128)) == sub((128, 128)), 1.0, 0.0).astype(BF)

    @pl.loop(first // 20, end // 20)
    def _(o):
        for u in range(20):
            wt[o * 20 + u] = lax.dot_general(eye, w[o * 20 + u], (((1,), (1,)), ((), ())), preferred_element_type=F32).astype(BF)


def build_oh(rows_v, cols_v, live, ohr, ohc):
    at = lane((1, SL))
    perm = jnp.where(sub((SL, SL)) == (at % (SL // 4)) * 4 + at // (SL // 4), 1.0, 0.0).astype(BF)
    ids = jnp.where(at < live, rows_v[...], -1).astype(F32)
    r = jnp.dot(jnp.broadcast_to(ids, (8, SL)).astype(BF), perm, preferred_element_type=F32)[0:1].astype(jnp.int32)
    c = jnp.where(at < live, cols_v[...], -1)

    def fill(oh, n, ids):
        @pl.loop(0, n // 32)
        def _(i):
            s = sub((32, SL)) + i * 32
            oh[pl.ds(pl.multiple_of(i * 32, 32), 32), :] = jnp.where(s == ids, 1.0, 0.0).astype(BF)

    fill(ohr, 256, r)
    fill(ohc, 512, c)


def table_b(x, tab):
    flat = tab.reshape(256 * 8, 128)
    i, j = sub((128, 512)), lane((128, 512))
    e = jnp.where(i == (j // 128) * 32 + j % 32, 1.0, 0.0).astype(BF)
    y = jnp.dot(x[...].reshape(512, 128), e, preferred_element_type=F32)
    for s in range(4):
        ys = y[:, s * 128:(s + 1) * 128].reshape(32, 16, 128)
        for par in range(2):
            flat[pl.ds(par * 4 + s, 256, stride=8), :] = ys[:, par * 8:par * 8 + 8].reshape(256, 128)


def table_a(d, tab):
    flat = tab.reshape(512 * 8, 128)
    for sp in range(2):
        x = d[:, :, sp * 128:(sp + 1) * 128].reshape(512, 128).astype(F32)
        xr = pltpu.roll(x, 64, 1)
        for s, par, v in ((2 * sp, 0, x), (2 * sp, 1, xr), (2 * sp + 1, 0, xr), (2 * sp + 1, 1, x)):
            flat[pl.ds(par * 4 + s, 512, stride=8), :] = v


def main(idx, tab, w, p, forward, unroll):
    grp = lane((8, 128)) // 32
    half = (lane((8, 128)) // 64) == (sub((8, 128)) // 4)

    pad = PAD if forward else 32
    zero = jnp.zeros((32, 128), BF)

    @pl.loop(0, SL // 8 // unroll)
    def _(o):
        lhs, out = [], []
        for u in range(unroll):
            ls = []
            for g in range(2):
                rs = []
                for k in range(4):
                    t = idx[0, (o * unroll + u) * 8 + g * 4 + k]
                    rs.append(jnp.where(half if forward else grp == k, tab[t], 0.0))
                v = jnp.concatenate(rs, 0).astype(BF)
                ls.append(jnp.concatenate([zero, v] if g else [v, zero], 1))
            lhs.append(jnp.concatenate(ls, 0))
        for u in range(unroll):
            rhs = w[pl.ds((o * unroll + u) * 2, 2)].reshape(256, 128)
            out.append(jnp.dot(lhs[u], rhs, preferred_element_type=F32))
        for u in range(unroll):
            for g in range(2):
                p[pl.ds(pl.multiple_of(((o * unroll + u) * 2 + g) * pad, 8), 32), :] = out[u][g * 32:g * 32 + 32]


def scatter_b(p, ohc, emit):
    low = lane((1, 128)) < 64
    for sp in range(2):
        fs = []
        for s in (2 * sp, 2 * sp + 1):
            m = jnp.where(low, p[pl.ds(s, SL, stride=8), :], p[pl.ds(4 + s, SL, stride=8), :])
            fs.append(m + pltpu.roll(m, 64, 1))
        x = jnp.where(low, fs[0], fs[1]).astype(BF)
        emit(sp, jnp.dot(ohc[...], x, preferred_element_type=F32))


def scatter_a(p, ohr, out):
    grp = lane((1, 128)) // 32
    halves = []
    for par in range(2):
        xs = []
        for k in range(4):
            x = None
            for s in range(4):
                m = p[pl.ds(k * 8 + par * 4 + s, SL // 4, stride=PAD), :]
                if s != k:
                    m = pltpu.roll(m, (32 * (s - k)) % 128, 1)
                x = m if s == 0 else jnp.where(grp == s, m, x)
            xs.append(x.astype(BF))
        y = jnp.dot(ohr[...], jnp.concatenate(xs, 0), preferred_element_type=F32)
        halves.append(y.reshape(32, 8, 128))
    out[...] = jnp.concatenate(halves, 1).astype(BF)


def wait_bytes(buf, n, sem):
    pltpu.make_async_copy(buf.at[pl.ds(0, n)], buf.at[pl.ds(0, n)], sem).wait()


def ring(n):
    return sorted(range(n), key=lambda d: -min(d, n - d))


def expand(x, width):
    e = jnp.where(sub((128, 4 * width)) // 32 == lane((128, 4 * width)) // width, 1.0, 0.0)
    return jnp.dot(x, e, precision=lax.Precision.HIGHEST, preferred_element_type=F32)


def rays_in(x, z, out):
    i, j = sub((128, 512)), lane((128, 512))
    g = j // 128
    e = jnp.where(i == (g // 2) * 64 + (j % 32) * 2 + g % 2, 1.0, 0.0)
    for b in range(4):
        y = jnp.dot(x[:, b * 128:(b + 1) * 128], e, precision=lax.Precision.HIGHEST, preferred_element_type=F32)
        for g in range(4):
            r = (g % 2) * 8 + b * 2 + g // 2
            z[r * 8:r * 8 + 8, :] = y[:, g * 128:(g + 1) * 128]
    grp = lane((1, 128)) // 32
    for h in range(2):
        v = z[pl.ds(h * 4, 16, stride=8), :]
        for s in range(1, 4):
            v = jnp.where(grp == s, z[pl.ds(h * 4 + s, 16, stride=8), :], v)
        out[h] = v


def rays_out(x, z, out):
    grp = lane((1, 128)) // 32
    for h in range(2):
        for s in range(4):
            v = jnp.where(grp == s, x[h], 0.0)
            v = v + pltpu.roll(v, 32, 1)
            z[pl.ds(h * 4 + s, 16, stride=8), :] = v + pltpu.roll(v, 64, 1)
    i, j = sub((128, 128)), lane((128, 128))
    e = jnp.where(i == (j // 64) * 64 + (j % 2) * 32 + (j % 64) // 2, 1.0, 0.0)
    for b in range(4):
        y = None
        for g in range(4):
            r = (g % 2) * 8 + b * 2 + g // 2
            v = z[r * 8:r * 8 + 8, :]
            y = v if g == 0 else jnp.where(grp == g, v, y)
        out[:, b * 128:(b + 1) * 128] = jnp.dot(y, e, precision=lax.Precision.HIGHEST, preferred_element_type=F32)


def pixels_part(x, h, z):
    low = lane((1, 128)) < 64
    for sp in range(2):
        v = x[:, sp * 128:(sp + 1) * 128]
        r = pltpu.roll(v, 64, 1)
        z[pl.ds(h * 4 + 2 * sp, 64, stride=8), :] = jnp.where(low, v, r)
        z[pl.ds(h * 4 + 2 * sp + 1, 64, stride=8), :] = jnp.where(low, r, v)


def pixels_out(z, out):
    low = lane((1, 128)) < 64
    for t in range(32):
        out[:, t * 128:(t + 1) * 128] = jnp.where(low, z[t * 16:t * 16 + 8, :], z[t * 16 + 8:t * 16 + 16, :])


def kernel(nr, nc, ny, rows_s, cols_s, rows_v, cols_v, count, t_hbm, sino, sol_o, res_o, grad_o,
           tv, st, w, wt, ohr, ohc, tb, ta, pb, pa,
           r_all, q0_all, q1_all, sr, sq, s1, g0_all, g1_all, pp, gp, rp, qp, sc,
           g_sh, r_sh, q_sh, zr, zs, zg, sems, tsem):
    i, j = lax.axis_index("rows"), lax.axis_index("cols")
    chunks = SL // CHUNK
    for k in range(chunks):
        tile_copy(t_hbm.at[0], tv, tsem, k).start()
    nx, nz = nr // 2, nc // ny
    x, core, z, y = i // 2, lax.rem(i, 2), j // ny, lax.rem(j, ny)
    cols = [lax.rem(z + dz, nz) * ny + lax.rem(y + dy, ny) for dz in ring(nz) for dy in ring(ny)][:-1]
    rows = [lax.rem(x + dx, nx) * 2 + (1 - core if dc else core) for dx in ring(nx) for dc in (1, 0)][:-1]
    barrier = pltpu.get_barrier_semaphore()
    for to in cols:
        pl.semaphore_signal(barrier, inc=1, device_id={"cols": to}, device_id_type=MESH)
    for to in rows:
        pl.semaphore_signal(barrier, inc=1, device_id={"rows": to}, device_id_type=MESH)

    def to_cols(src, dst, ph, h):
        for to in cols:
            pltpu.make_async_remote_copy(src(to), dst.at[j], sems.at[0, ph, h], sems.at[1, ph, h], device_id={"cols": to}, device_id_type=MESH).start()

    def to_rows(src, dst, ph, h):
        for to in rows:
            pltpu.make_async_remote_copy(src(to), dst.at[i], sems.at[0, ph, h], sems.at[1, ph, h], device_id={"rows": to}, device_id_type=MESH).start()

    def arrived(buf, n, ph, h):
        wait_bytes(buf, n - 1, sems.at[1, ph, h])

    def left(buf, n, ph, h):
        wait_bytes(buf, n - 1, sems.at[0, ph, h])

    rays_in(sino[...], zr, r_sh)
    for h in range(2):
        r_all[h, j] = r_sh[h].astype(BF)
    build_oh(rows_v, cols_v, count[0, 0], ohr, ohc)
    pl.semaphore_wait(barrier, nc + nr - 2)
    for h in range(2):
        to_cols(lambda to: r_all.at[h, j], r_all.at[h], 0, h)

    for k in range(chunks):
        tile_copy(t_hbm.at[0], tv, tsem, k).wait()

    @pl.loop(0, chunks)
    def _(k):
        build_w(tv, st, w, k)

    def back(h, src):
        table_b(src.at[h], tb)
        main(rows_s, tb, w, pb, False, 20)

    def sums_of(to):
        def emit(sp, y):
            to[:, sp * 128:(sp + 1) * 128] = y

        scatter_b(pb, ohc, emit)

    def spread_pair(h, n, ph, sp, y):
        at = pl.ds(sp * 128, 128)
        parts, buf = pp.at[n, h], gp.at[n, h]
        parts[:, :, at] = y.astype(BF).reshape(nr, 64, 128)
        to_rows(lambda to: parts.at[to, :, at], buf.at[:, :, at], ph, h)

    def spread(h, n, ph, sums):
        for sp in range(2):
            spread_pair(h, n, ph, sp, sums[:, sp * 128:(sp + 1) * 128])
        gp[n, h, i] = pp[n, h, i]

    def forward(h, n, ph, d_all):
        table_a(d_all, ta)
        main(cols_s, ta, wt, pa, True, 20)
        parts, buf = rp.at[n, h], qp.at[n, h]
        scatter_a(pa, ohr, parts)
        to_cols(lambda to: parts.at[to], buf, ph, h)
        buf[j] = parts[j]

    def total(buf, n, ph, h):
        arrived(buf, n, ph, h)
        return jnp.sum(buf[...].astype(F32), 0)

    def exchange(n, h, vals, ph):
        vals = [jnp.sum(v.reshape(-1, 128), 0, keepdims=True) for v in vals]
        buf = sc.at[n, h]
        buf[i] = jnp.concatenate(vals + [jnp.zeros((8 - len(vals), 128), F32)], 0)
        to_rows(lambda to: buf.at[i], buf, ph, h)

    def exchanged(n, h, ph):
        tot = total(sc.at[n, h], nr, ph, h)
        return expand(tot, 32), expand(tot, 64)

    @pl.loop(0, 2)
    def _(h):
        arrived(r_all.at[h], nc, 0, h)
        back(h, r_all)

        def emit(sp, y):
            sr[h, :, sp * 128:(sp + 1) * 128] = y
            spread_pair(h, 0, 1, sp, y)

        scatter_b(pb, ohc, emit)
        gp[0, h, i] = pp[0, h, i]
    build_wt(w, wt, 0, 80)
    for h in range(2):
        g = total(gp.at[0, h], nr, 1, h)
        g0_all[h, i] = g.astype(BF)
        to_rows(lambda to: g0_all.at[h, i], g0_all.at[h], 2, h)
        g_sh[h] = g
    build_wt(w, wt, 80, 160)
    @pl.loop(0, 2)
    def _(h):
        arrived(g0_all.at[h], nr, 2, h)
        forward(h, 0, 3, g0_all.at[h])
    for h in range(2):
        q = total(qp.at[0, h], nc, 3, h)
        q0_all[h, j] = q.astype(BF)
        to_cols(lambda to: q0_all.at[h, j], q0_all.at[h], 4, h)
        q_sh[h] = q
    n32, n64 = [None, None], [None, None]

    def norms0(h):
        arrived(q0_all.at[h], nc, 4, h)
        r0, q0 = r_all[h].astype(F32), q0_all[h].astype(F32)
        exchange(0, h, [r0 * q0, q0 * q0], 5)

    def step0(h):
        n32[h], n64[h] = exchanged(0, h, 5)
        v = sr[h] - n64[h][0:1] / (n64[h][1:2] + EPS) * sq[h]
        spread(h, 1, 6, v)
        sr[h] = v

    norms0(0)
    back(0, q0_all)
    sums_of(sq.at[0])
    norms0(1)
    step0(0)
    back(1, q0_all)
    sums_of(sq.at[1])
    step0(1)
    for h in range(2):
        r_sh[h] = r_sh[h] - n32[h][0:1] / (n32[h][1:2] + EPS) * q_sh[h]
    for h in range(2):
        g = total(gp.at[1, h], nr, 6, h)
        g1_all[h, i] = g.astype(BF)
        to_rows(lambda to: g1_all.at[h, i], g1_all.at[h], 7, h)
        zg[h] = g
    @pl.loop(0, 2)
    def _(h):
        arrived(g1_all.at[h], nr, 7, h)
        forward(h, 1, 8, g1_all.at[h])
    for h in range(2):
        q = total(qp.at[1, h], nc, 8, h)
        q1_all[h, j] = q.astype(BF)
        to_cols(lambda to: q1_all.at[h, j], q1_all.at[h], 9, h)
        zs[h] = q

    def norms1(h):
        arrived(q1_all.at[h], nc, 9, h)
        r0, q0, q1 = r_all[h].astype(F32), q0_all[h].astype(F32), q1_all[h].astype(F32)
        exchange(1, h, [r0 * q1, q1 * q1, q1 * q0], 10)

    def scalars(n, m):
        alpha = n[0:1] / (n[1:2] + EPS)
        gamma = m[0:1] - alpha * m[2:3]
        beta = gamma / (n[0:1] + EPS)
        delta = m[1:2] + 2.0 * beta * m[2:3] + beta * beta * n[1:2]
        return alpha, beta, gamma / (delta + EPS)

    m32, m64 = [None, None], [None, None]

    def step1(h):
        m32[h], m64[h] = exchanged(1, h, 10)
        _, beta, alpha = scalars(n64[h], m64[h])
        spread(h, 2, 11, sr[h] - alpha * (s1[...] + beta * sq[h]))

    norms1(0)
    back(0, q1_all)
    sums_of(s1)
    norms1(1)
    step1(0)
    back(1, q1_all)
    sums_of(s1)
    step1(1)
    for h in range(2):
        _, beta, alpha = scalars(n32[h], m32[h])
        r_sh[h] = r_sh[h] - alpha * (zs[h] + beta * q_sh[h])
        alpha0, beta, alpha = scalars(n64[h], m64[h])
        pixels_part(alpha0 * g_sh[h] + alpha * (zg[h] + beta * g_sh[h]), h, zr)
    pixels_out(zr, sol_o)
    rays_out(r_sh, zr, res_o)
    for h in range(2):
        pixels_part(total(gp.at[2, h], nr, 11, h), h, zr)
    pixels_out(zr, grad_o)
    for h in range(2):
        for ph, buf, n in ((0, r_all, nc), (1, gp.at[0], nr), (2, g0_all, nr), (3, qp.at[0], nc), (4, q0_all, nc), (5, sc.at[0], nr), (6, gp.at[1], nr),
                           (7, g1_all, nr), (8, qp.at[1], nc), (9, q1_all, nc), (10, sc.at[1], nr), (11, gp.at[2], nr)):
            left(buf.at[h], n, ph, h)


def write(a, b, c, x, y, z):
    x[...] = a[...]
    y[...] = b[...]
    z[...] = c[...]


def solution(mesh):
    nr, nc = mesh.shape["rows"], mesh.shape["cols"]
    ny = 4

    def body(sinogram, tiles, tile_rows, tile_cols, tile_counts):
        vm, sm = pl.BlockSpec(memory_space=pltpu.VMEM), pl.BlockSpec(memory_space=pltpu.SMEM)

        def ray(n, t=BF):
            return pltpu.VMEM((*n, nc, 16, 128), t)

        def pix(n):
            return pltpu.VMEM((*n, nr, 64, 256), BF)

        outs = (jax.ShapeDtypeStruct((8, 4096), F32), jax.ShapeDtypeStruct((8, 512), F32), jax.ShapeDtypeStruct((8, 4096), F32))
        made = pl.pallas_call(
            functools.partial(kernel, nr, nc, ny),
            out_shape=outs,
            in_specs=[sm, sm, vm, vm, sm, pl.BlockSpec(memory_space=pl.ANY), vm],
            out_specs=(vm, vm, vm),
            scratch_shapes=[
                pltpu.VMEM((SL // CHUNK, CHUNK, 4096), BF), pltpu.VMEM((2, CHUNK * PAD, 128), F32),
                pltpu.VMEM((160, 128, 128), BF), pltpu.VMEM((160, 128, 128), BF),
                pltpu.VMEM((256, SL), BF), pltpu.VMEM((512, SL), BF), pltpu.VMEM((256, 8, 128), F32), pltpu.VMEM((512, 8, 128), F32),
                pltpu.VMEM((SL * 8, 128), F32), pltpu.VMEM((160 * PAD, 128), F32),
                ray((2,)), ray((2,)), ray((2,)), pltpu.VMEM((2, 512, 256), F32), pltpu.VMEM((2, 512, 256), F32), pltpu.VMEM((512, 256), F32),
                pix((2,)), pix((2,)), pix((3, 2)), pix((3, 2)), ray((2, 2)), ray((2, 2)), pltpu.VMEM((2, 2, nr, 8, 128), F32),
                pltpu.VMEM((2, 64, 256), F32), pltpu.VMEM((2, 16, 128), F32), pltpu.VMEM((2, 16, 128), F32),
                pltpu.VMEM((512, 128), F32), pltpu.VMEM((2, 16, 128), F32), pltpu.VMEM((2, 64, 256), F32),
                pltpu.SemaphoreType.DMA((2, 12, 2)), pltpu.SemaphoreType.DMA((SL // CHUNK,)),
            ],
            compiler_params=pltpu.CompilerParams(collective_id=0, has_side_effects=True, vmem_limit_bytes=60 * 2**20),
            name="cgls",
        )(tile_rows, tile_cols, tile_rows, tile_cols, tile_counts, tiles, sinogram)
        return pl.pallas_call(
            write,
            out_shape=outs,
            in_specs=[vm] * 3,
            out_specs=(vm,) * 3,
            name="write",
        )(*made)

    return jax.shard_map(
        body,
        mesh=mesh,
        in_specs=(
            P(None, ("rows", "cols")),
            P("rows", "cols", None),
            P("rows", "cols"),
            P("rows", "cols"),
            P("rows", "cols"),
        ),
        out_specs=(P(None, ("cols", "rows")), P(None, ("rows", "cols")), P(None, ("cols", "rows"))),
        check_vma=False,
    )
```
